32 devices in a mesh: pole: 4 (over y, x), dom: 8 (over z, core).
Axes of the slice: x: 2, y: 2, z: 4, core: 2. Of those that a mesh axis runs over, the one named last changes fastest.
Arguments:
- y_interior: float32 [8, 512, 256], P('dom', 'pole'), may hold values from -6 to 6
- y_separator: float32 [8, 64, 256], P('dom'), may hold values from -6 to 6
- green: float32 [2, 4, 8, 512, 512], P(None, 'pole', 'dom'), as said below
- pole_data: float32 [4, 4], P(None, 'pole'), as said below
- coupling: float32 [8, 2, 64, 128], P('dom')
- sep_block: float32 [8, 64, 64], P('dom'), as said below
- iface_rows: int32 [8, 2, 128], P('dom'), may hold values from 0 to 511, as said below
Outputs:
- filtered: float32 [8, 512, 256], P('dom', 'pole')
- filtered_sep: float32 [8, 64, 256], P('dom', 'pole')
The draws below stay inside these ranges and needn't reach their ends.
Inputs may be any that keep to these rules, and one draw needn't show every extreme that they name: green[:, p, d] holds the real and imaginary parts of the inverse of z[p] I - H[d], where H[d] is a real symmetric matrix of order 512 and z[p] is the pole of pole_data. `pole_data`: every pole lies in the upper half plane with imaginary part 0.3 or more. `sep_block`: each block is symmetric. iface_rows[d, 0] and iface_rows[d, 1] each list 128 distinct rows of domain d, and no row is in both.
All inputs are finite; a program needn't handle non-finite values.
Results may differ from the reference program's by a relative error of at most 0.00095.
Values sent between devices are 32-bit elements; how exact they have to be, the bound alone decides.
A program may use at most 64 MiB of HBM per device.

```python
import math
import jax
import jax.numpy as jnp
from jax import lax

NI = 512
S = 64
B = 128
M = 256
POLES = 4
DOMAINS = 8


dimer_hop = 24.0


edge_spread = 0.5


bulk_link = 0.5


couple_gain = 12.0


def pole_table(key):
    pole_key = jax.random.fold_in(key, 101)
    pole_keys = jax.random.split(pole_key, 4)
    center = jax.random.uniform(pole_keys[0], (), jnp.float32, -0.4, 0.4)
    radius = jax.random.uniform(pole_keys[1], (), jnp.float32, 1.3, 1.7)
    height = radius * jax.random.uniform(pole_keys[2], (), jnp.float32, 0.8, 1.2)
    spacing = 0.76 * math.pi / POLES
    jitter = jax.random.uniform(pole_keys[3], (POLES,), jnp.float32, 0.2, 0.8)
    angles = 0.12 * math.pi + spacing * (jnp.arange(POLES, dtype=jnp.float32) + jitter)
    real_part = center + radius * jnp.cos(angles)
    imag_part = height * jnp.sin(angles)
    weight_real = spacing / math.pi * height * jnp.cos(angles)
    weight_imag = spacing / math.pi * radius * jnp.sin(angles)
    return jnp.stack([real_part, imag_part, weight_real, weight_imag])


def iface_ranking(key):
    row_key = jax.random.fold_in(key, 404)
    positions = jnp.arange(NI, dtype=jnp.int32)[None, :]
    domain_ids = jnp.arange(DOMAINS, dtype=jnp.int32)[:, None]
    scores = jax.random.randint(row_key, (DOMAINS, NI), 0, 1 << 20, dtype=jnp.int32) * NI + positions
    end_rows = (positions == 0) | (positions == NI - 1)
    scores = jnp.where((domain_ids == 0) & end_rows, -1 - positions, scores)
    scores = jnp.where((domain_ids == 1) & end_rows, (1 << 30) + positions, scores)
    return jnp.argsort(scores, axis=1).astype(jnp.int32)


def draw_pole_data(key, part):
    return pole_table(key)


def draw_green(key, part):
    pole_rows = pole_table(key)
    ranking = iface_ranking(key)
    matrix_key = jax.random.fold_in(key, 202)
    noise_draw = jax.random.normal(matrix_key, (DOMAINS, NI, NI), jnp.float32)
    symmetric = (noise_draw + jnp.swapaxes(noise_draw, 1, 2)) / jnp.sqrt(2.0)
    positions = jnp.arange(NI, dtype=jnp.int32)
    in_first = positions < B
    in_last = positions >= NI - B
    in_edge = in_first | in_last
    in_bulk = jnp.logical_not(in_edge)
    edge_scale = edge_spread / math.sqrt(B)
    bulk_scale = 1.0 / math.sqrt(max(NI - 2 * B, 1))
    link_scale = bulk_link / math.sqrt(NI)
    same_side = in_first[:, None] & in_first[None, :] | in_last[:, None] & in_last[None, :]
    both_bulk = in_bulk[:, None] & in_bulk[None, :]
    mixed = in_edge[:, None] & in_bulk[None, :] | in_bulk[:, None] & in_edge[None, :]
    scale_table = (jnp.where(same_side, edge_scale, 0.0) + jnp.where(both_bulk, bulk_scale, 0.0) + jnp.where(mixed, link_scale, 0.0)).astype(jnp.float32)
    paired = (positions[None, :] == positions[:, None] + (NI - B)) & in_first[:, None]
    dimer = jnp.where(paired | paired.T, dimer_hop, 0.0).astype(jnp.float32)
    canonical = symmetric * scale_table[None] + dimer[None]
    eigen_values, canon_vectors = jnp.linalg.eigh(canonical)
    inverse = jnp.argsort(ranking, axis=1).astype(jnp.int32)
    eigen_vectors = jnp.take_along_axis(canon_vectors, inverse[:, :, None], axis=1)
    offset = pole_rows[0][:, None, None] - eigen_values[None]
    denominator = offset * offset + pole_rows[1][:, None, None] ** 2
    real_weight = offset / denominator
    imag_weight = -pole_rows[1][:, None, None] / denominator
    green_real = jnp.einsum('dik,pdk,djk->pdij', eigen_vectors, real_weight, eigen_vectors)
    green_imag = jnp.einsum('dik,pdk,djk->pdij', eigen_vectors, imag_weight, eigen_vectors)
    return jnp.stack([green_real, green_imag]).astype(jnp.float32)


def draw_coupling(key, part):
    couple_key = jax.random.fold_in(key, 505)
    values = jax.random.normal(couple_key, (DOMAINS, 2, S, B), jnp.float32)
    return (values * (couple_gain / math.sqrt(B))).astype(jnp.float32)


def draw_sep_block(key, part):
    block_key = jax.random.fold_in(key, 303)
    noise_draw = jax.random.normal(block_key, (DOMAINS, S, S), jnp.float32)
    return (noise_draw + jnp.swapaxes(noise_draw, 1, 2)) / jnp.sqrt(2.0 * S)


def draw_iface_rows(key, part):
    ranking = iface_ranking(key)
    return jnp.stack([ranking[:, :B], ranking[:, NI - B:]], axis=1).astype(jnp.int32)


def steps_of(own_key, dims, cuts, smallest, top_value):
    gain = 1.0
    for dim, blocks in cuts:
        draws = jax.random.uniform(jax.random.fold_in(jax.random.fold_in(own_key, 6), dim), (blocks,), jnp.float32, smallest / len(cuts), top_value / len(cuts))
        gain = gain * jnp.repeat(jnp.exp(draws), dims[dim] // blocks).reshape((-1,) + (1,) * (len(dims) - 1 - dim))
    return gain


def noise(key, extent, scale, most, cuts=(), kind=jnp.bfloat16):
    array = scale * jax.random.normal(key, extent, jnp.float32)
    if cuts:
        array = array * steps_of(key, extent, cuts, -0.22, 0.18)
    return jnp.clip(array, -most, most).astype(kind)


def setup_inputs(seed: int = 0) -> dict:
    streams_of = jax.random.split(jax.random.key(seed), 8)
    return {
        "y_interior": noise(streams_of[0], (DOMAINS, NI, M), 1.0, 6.0, ((0, 8), (1, 4)), jnp.float32),
        "y_separator": noise(streams_of[1], (DOMAINS, S, M), 1.0, 6.0, ((0, 8),), jnp.float32),
        "green": draw_green(jax.random.fold_in(streams_of[7], 71), 0),
        "pole_data": draw_pole_data(jax.random.fold_in(streams_of[7], 71), 0),
        "coupling": draw_coupling(jax.random.fold_in(streams_of[7], 71), 0),
        "sep_block": draw_sep_block(jax.random.fold_in(streams_of[7], 71), 0),
        "iface_rows": draw_iface_rows(jax.random.fold_in(streams_of[7], 71), 0),
    }


precise_mode = lax.Precision.HIGHEST

def matmul(left_side, right_side):
    return jnp.matmul(left_side, right_side, precision=precise_mode)

def complex_mul(left_factor, right_factor):
    return jnp.stack([matmul(left_factor[0], right_factor[0]) - matmul(left_factor[1], right_factor[1]), matmul(left_factor[0], right_factor[1]) + matmul(left_factor[1], right_factor[0])])

def real_left(real_mat, right_factor):
    return jnp.stack([matmul(real_mat, right_factor[0]), matmul(real_mat, right_factor[1])])

def real_right(left_factor, real_mat):
    return jnp.stack([matmul(left_factor[0], real_mat), matmul(left_factor[1], real_mat)])

def complex_solve(pivot_blk, right_hand):
    sep_order = pivot_blk.shape[-1]
    upper_half = jnp.concatenate([pivot_blk[0], -pivot_blk[1]], axis=1)
    lower_half = jnp.concatenate([pivot_blk[1], pivot_blk[0]], axis=1)
    system = jnp.concatenate([upper_half, lower_half], axis=0)
    stacked = jnp.concatenate([right_hand[0], right_hand[1]], axis=0)
    normal_matrix = matmul(system.T, system)
    factor = jnp.linalg.cholesky(normal_matrix)
    solved = jax.scipy.linalg.cho_solve((factor, True), matmul(system.T, stacked))
    return jnp.stack([solved[:sep_order], solved[sep_order:]])

def chain_solve(pivots, lowers, uppers, rights):
    sep_width = pivots.shape[-1]

    def forward(carry, chain_items):
        prev_coupled, prev_partial = carry
        pivot_blk, lower_blk, upper_blk, right_blk = chain_items
        reduced = pivot_blk - complex_mul(lower_blk, prev_coupled)
        adjusted = right_blk - complex_mul(lower_blk, prev_partial)
        solved = complex_solve(reduced, jnp.concatenate([upper_blk, adjusted], axis=-1))
        result = (solved[:, :, :sep_width], solved[:, :, sep_width:])
        return (result, result)
    initial = (jnp.zeros(pivots.shape[1:], jnp.float32), jnp.zeros(rights.shape[1:], jnp.float32))
    unused, (coupled, partial_sol) = lax.scan(forward, initial, (pivots, lowers, uppers, rights))

    def backward(following, chain_items):
        coupled_blk, partial_blk = chain_items
        current = partial_blk - complex_mul(coupled_blk, following)
        return (current, current)
    unused_last, solutions = lax.scan(backward, jnp.zeros(rights.shape[1:], jnp.float32), (coupled, partial_sol), reverse=True)
    return solutions

def domain_pieces(green_dom, interior_v, coupling_dom, rows_dom):
    right_rows = rows_dom[0]
    left_rows = rows_dom[1]
    right_map = coupling_dom[0]
    left_map = coupling_dom[1]
    inner_u = real_right(jnp.take(green_dom, right_rows, axis=2), right_map.T)
    inner_w = real_right(jnp.take(green_dom, left_rows, axis=2), left_map.T)
    own_pivot = real_left(right_map, jnp.take(inner_u, right_rows, axis=1))
    own_lower = -real_left(right_map, jnp.take(inner_w, right_rows, axis=1))
    own_right = real_left(right_map, jnp.take(interior_v, right_rows, axis=1))
    next_pack = jnp.concatenate([real_left(left_map, jnp.take(inner_w, left_rows, axis=1)), real_left(left_map, jnp.take(inner_u, left_rows, axis=1)), real_left(left_map, jnp.take(interior_v, left_rows, axis=1))], axis=-1)
    return (inner_u, inner_w, own_pivot, own_lower, own_right, next_pack)

def reference(y_interior, y_separator, green, pole_data, coupling, sep_block, iface_rows):
    domains = y_interior.shape[0]
    poles = pole_data.shape[1]
    sep_order = sep_block.shape[-1]
    identity = jnp.eye(sep_order, dtype=jnp.float32)
    not_first = (jnp.arange(domains, dtype=jnp.int32) > 0).astype(jnp.float32)[:, None, None, None]
    separator_rhs = jnp.stack([y_separator, jnp.zeros_like(y_separator)], axis=1)
    separator_own = jnp.stack([sep_block, jnp.zeros_like(sep_block)], axis=1)

    def per_pole(totals, pole_index):
        column = pole_data[:, pole_index]

        def per_domain(domain_index):
            green_dom = green[:, pole_index, domain_index]
            interior_v = real_right(green_dom, y_interior[domain_index])
            return (interior_v,) + domain_pieces(green_dom, interior_v, coupling[domain_index], iface_rows[domain_index])
        interior_v, inner_u, inner_w, own_pivot, own_lower, own_right, next_pack = lax.map(per_domain, jnp.arange(domains, dtype=jnp.int32))
        shifted = jnp.concatenate([next_pack[1:], jnp.zeros_like(next_pack[:1])], axis=0)
        shift_eye = jnp.stack([column[0] * identity, column[1] * identity])
        pivots = shift_eye[None] - separator_own - own_pivot - shifted[..., :sep_order]
        uppers = -shifted[..., sep_order:2 * sep_order]
        rights = separator_rhs + own_right + shifted[..., 2 * sep_order:]
        lowers = own_lower * not_first
        solutions = chain_solve(pivots, lowers, uppers, rights)
        previous = jnp.concatenate([jnp.zeros_like(solutions[:1]), solutions[:-1]], axis=0)
        field_value = interior_v + jax.vmap(complex_mul)(inner_u, solutions) + jax.vmap(complex_mul)(inner_w, previous)
        weighted = column[2] * field_value[:, 0] - column[3] * field_value[:, 1]
        weighted_sep = column[2] * solutions[:, 0] - column[3] * solutions[:, 1]
        return ((totals[0] + weighted, totals[1] + weighted_sep), None)
    initial = (jnp.zeros(y_interior.shape, jnp.float32), jnp.zeros(y_separator.shape, jnp.float32))
    (filtered, filtered_sep), unused = lax.scan(per_pole, initial, jnp.arange(poles, dtype=jnp.int32))
    return (filtered, filtered_sep)
```

```python
import functools
import jax
import jax.numpy as jnp
from jax import lax
from jax.experimental import pallas as pl
from jax.experimental.pallas import tpu as pltpu
from jax.sharding import PartitionSpec as P

MESH = pl.DeviceIdType.MESH
f32 = jnp.float32


def dot(a, b, ca=1, cb=0):
    return lax.dot_general(
        a, b, (((ca,), (cb,)), ((), ())), precision=lax.Precision.HIGHEST, preferred_element_type=f32
    )


def lanes_below(shape, limit):
    return lax.broadcasted_iota(jnp.int32, shape, 1) < limit


def swap(value, half):
    return pltpu.roll(value, half, 1)


def small_inverse(dr, di):
    n = len(dr)
    row = lax.broadcasted_iota(jnp.int32, dr[0].shape, 0)
    for k in range(n):
        pr, pi = dr[k][k : k + 1], di[k][k : k + 1]
        scale = 1.0 / (pr * pr + pi * pi)
        qr, qi = pr * scale, -pi * scale
        here = row == k
        cr, ci = dr[k], di[k]
        new_r, new_i = [], []
        for m in range(n):
            if m == k:
                new_r.append(jnp.where(here, qr, ci * qi - cr * qr))
                new_i.append(jnp.where(here, qi, -(cr * qi + ci * qr)))
            else:
                tr, ti = dr[m][k : k + 1], di[m][k : k + 1]
                rr, ri = tr * qr - ti * qi, tr * qi + ti * qr
                new_r.append(jnp.where(here, rr, dr[m] - cr * rr + ci * ri))
                new_i.append(jnp.where(here, ri, di[m] - cr * ri - ci * rr))
        dr, di = new_r, new_i
    return dr, di


def inverse(packed):
    n = packed.shape[0]
    step = 8
    lane = lax.broadcasted_iota(jnp.int32, packed.shape, 1)
    within = lax.rem(lane, n)
    swept = within < step
    sign = jnp.where(lane[:step] < n, -1.0, 1.0)
    unit = (lane[:step] == lax.broadcasted_iota(jnp.int32, (step, 2 * n), 0)).astype(f32)

    def body(_, a):
        shape = a.shape
        col_r = [jnp.broadcast_to(a[:, m : m + 1], shape) for m in range(step)]
        col_i = [jnp.broadcast_to(a[:, n + m : n + m + 1], shape) for m in range(step)]
        inv_r, inv_i = small_inverse([c[:step] for c in col_r], [c[:step] for c in col_i])
        top = jnp.where(swept[:step], unit, a[:step])
        turned = swap(top, n) * sign
        r = jnp.zeros_like(top)
        ri = jnp.zeros_like(top)
        for m in range(step):
            tm, um = top[m : m + 1], turned[m : m + 1]
            r = r + inv_r[m] * tm + inv_i[m] * um
            ri = ri + inv_r[m] * um - inv_i[m] * tm
        rest = jnp.where(swept[step:], 0.0, a[step:])
        for m in range(step):
            rest = rest - col_r[m][step:] * r[m : m + 1] - col_i[m][step:] * ri[m : m + 1]
        full = jnp.concatenate([rest, r], axis=0)
        return jnp.where(within < n - step, pltpu.roll(full, 2 * n - step, 1), pltpu.roll(full, n - step, 1))

    return lax.fori_loop(0, n // step, body, packed)


def embed(re, im):
    return jnp.concatenate(
        [jnp.concatenate([re, im], axis=1), jnp.concatenate([-im, re], axis=1)], axis=0
    )


def embed_packed(packed):
    n = packed.shape[1] // 2
    turned = swap(packed, n) * jnp.where(lanes_below(packed.shape, n), -1.0, 1.0)
    return jnp.concatenate([packed, turned], axis=0)


def kernel(
    poles, doms, y_ref, ysep_ref, green_ref, pole_ref, coup_ref, sep_ref, rows_ref,
    out_ref, outsep_ref,
    ybuf, part, part_sep, got, got_sep, sbuf, sgot, tbufs, tgots, xsends, xgots, first, maps,
    y_s, y_r, s_s, s_r, t_s, t_r, x_s, x_r, o_s, o_r, p_s, p_r,
):
    levels = doms.bit_length() - 1
    pole = lax.axis_index("pole")
    dom = lax.axis_index("dom")
    bits = [lax.rem(lax.div(dom, 1 << l), 2) for l in range(levels)]
    mates = [dom + (1 - 2 * bits[l]) * (1 << l) for l in range(levels)]
    peers = [lax.rem(pole + o, poles) for o in range(1, poles)]

    def send(src, dst, send_sem, recv_sem, place):
        copy = pltpu.make_async_remote_copy(
            src_ref=src, dst_ref=dst, send_sem=send_sem, recv_sem=recv_sem,
            device_id=place, device_id_type=MESH,
        )
        copy.start()
        return copy

    barrier = pltpu.get_barrier_semaphore()
    for peer in peers:
        pl.semaphore_signal(barrier, inc=1, device_id=(peer, dom), device_id_type=MESH)
    for mate in mates:
        pl.semaphore_signal(barrier, inc=1, device_id=(pole, mate), device_id_type=MESH)
    pl.semaphore_wait(barrier, len(peers) + len(mates))

    sent = []
    y_copies = [
        send(y_ref, ybuf.at[pole], y_s.at[o], y_r.at[o], (peer, dom)) for o, peer in enumerate(peers)
    ]
    ybuf[pole] = y_ref[...]

    s = sep_ref.shape[0]
    ni = green_ref.shape[1]
    m = y_ref.shape[1]
    zr, zi, wr, wi = pole_ref[0], pole_ref[1], pole_ref[2], pole_ref[3]
    spot = lax.broadcasted_iota(jnp.int32, (rows_ref.shape[1], ni), 1)
    pick_u = (rows_ref[0] == spot).astype(f32)
    pick_w = (rows_ref[1] == spot).astype(f32)
    has_left = (dom > 0).astype(f32)
    c = jnp.concatenate([dot(coup_ref[1] * has_left, pick_w), dot(coup_ref[0], pick_u)], axis=0)
    n_r = dot(c, green_ref[0])
    n_i = dot(c, green_ref[1])
    k_r = dot(n_r, c, 1, 1)
    k_i = dot(n_i, c, 1, 1)
    eye = (
        lax.broadcasted_iota(jnp.int32, (s, s), 0) == lax.broadcasted_iota(jnp.int32, (s, s), 1)
    ).astype(f32)
    gap = jnp.zeros((s, s), f32)
    corner_r = zr * eye - sep_ref[...]
    corner_i = zi * eye

    def place_corner(block):
        low = jnp.concatenate([gap, block], axis=1)
        return jnp.concatenate([jnp.zeros_like(low), low], axis=0)

    own = jnp.concatenate([place_corner(corner_r) - k_r, place_corner(corner_i) - k_i], axis=1)
    sbuf[0] = own
    s_copies = [send(sbuf.at[0], sgot.at[0], s_s.at[0], s_r.at[0], (pole, mates[0]))]

    maps[:, : 2 * s] = jnp.transpose(wr * n_r - wi * n_i)
    maps[:, 2 * s :] = jnp.transpose(-(wr * n_i + wi * n_r))

    for copy in y_copies:
        copy.wait_recv()
    y_all = ybuf[...].reshape(ni, m)
    right_r = jnp.transpose(dot(n_r, y_all))
    right_i = jnp.transpose(dot(n_i, y_all))
    sep_t = jnp.transpose(jnp.concatenate([jnp.zeros((s, m), f32), ysep_ref[...]], axis=0))
    t = jnp.concatenate([right_r + sep_t, right_i], axis=1)

    low = lanes_below((s, 2 * s), s)
    kept = []
    t_copies = []
    for l in range(levels):
        width = t.shape[0] // 2
        tbufs[l][0] = t[:width]
        tbufs[l][1] = t[width:]
        t_copies.append(
            send(tbufs[l].at[1 - bits[l]], tgots[l], t_s.at[l], t_r.at[l], (pole, mates[l]))
        )
        if l == 0:
            weighted = wr * green_ref[0] - wi * green_ref[1]
            first[...] = dot(weighted, y_all)
        is_low = bits[l] == 0
        s_copies[l].wait_recv()
        mine, other = sbuf[l], sgot[l]
        left = jnp.where(is_low, mine, other)
        right = jnp.where(is_low, other, mine)
        lr, li = left[:, : 2 * s], left[:, 2 * s :]
        rr, ri = right[:, : 2 * s], right[:, 2 * s :]
        p_r_ = swap(lr[s:], s) + rr[:s]
        p_i_ = swap(li[s:], s) + ri[:s]
        pivot = jnp.where(low, p_r_, swap(p_i_, s))
        y_re = jnp.where(low, lr[s:], rr[:s])
        y_im = jnp.where(low, li[s:], ri[:s])
        turned = jnp.transpose(jnp.concatenate([y_re, y_im], axis=0))
        pinv = inverse(pivot)
        z = dot(pinv, embed(y_re, y_im))
        z_re, z_im = z[:, : 2 * s], z[:, 2 * s :]
        z_emb = embed(z_re, z_im)
        base = jnp.concatenate(
            [
                jnp.concatenate([jnp.where(low, lr[:s], 0.0), jnp.where(low, li[:s], 0.0)], axis=1),
                jnp.concatenate([jnp.where(low, 0.0, rr[s:]), jnp.where(low, 0.0, ri[s:])], axis=1),
            ],
            axis=0,
        )
        merged = base - dot(turned, z_emb)
        if l + 1 < levels:
            sbuf[l + 1] = merged
            s_copies.append(
                send(sbuf.at[l + 1], sgot.at[l + 1], s_s.at[l + 1], s_r.at[l + 1], (pole, mates[l + 1]))
            )
        t_copies[l].wait_recv()
        t_mine, t_other = tbufs[l][bits[l]], tgots[l][...]
        t_left = jnp.where(is_low, t_mine, t_other)
        t_right = jnp.where(is_low, t_other, t_mine)
        below = lanes_below((width, 2 * s), s)
        sum_r = swap(t_left[:, : 2 * s], s) + t_right[:, : 2 * s]
        sum_i = swap(t_left[:, 2 * s :], s) + t_right[:, 2 * s :]
        middle = jnp.where(below, sum_r, swap(sum_i, s))
        ends = jnp.concatenate(
            [
                jnp.where(below, t_left[:, : 2 * s], t_right[:, : 2 * s]),
                jnp.where(below, t_left[:, 2 * s :], t_right[:, 2 * s :]),
            ],
            axis=1,
        )
        t = ends - dot(middle, z_emb)
        back = jnp.concatenate(
            [jnp.concatenate([z_re, -z_im], axis=1), jnp.concatenate([z_im, z_re], axis=1)], axis=0
        )
        kept.append((dot(middle, embed_packed(pinv)), back, below))

    width = t.shape[0]
    below = lanes_below((width, 2 * s), s)
    pivot = jnp.where(low, swap(merged[s:, : 2 * s], s), merged[s:, 2 * s :])
    rhs = jnp.where(below, swap(t[:, : 2 * s], s), t[:, 2 * s :])
    x_end = dot(rhs, embed_packed(inverse(pivot)))
    x = jnp.concatenate(
        [jnp.where(below, 0.0, swap(x_end, s)), jnp.where(below, 0.0, x_end)], axis=1
    )
    x_copies = []
    for l in reversed(range(levels)):
        part_m, back, below = kept[l]
        xm = part_m - dot(x, back, 1, 1)
        xr, xi = x[:, : 2 * s], x[:, 2 * s :]
        xm_t = swap(xm, s)
        x_left = jnp.concatenate([jnp.where(below, xr, xm_t), jnp.where(below, xi, xm)], axis=1)
        x_right = jnp.concatenate([jnp.where(below, xm, xr), jnp.where(below, xm_t, xi)], axis=1)
        is_low = bits[l] == 0
        xsends[l][...] = jnp.where(is_low, x_right, x_left)
        copy = send(xsends[l], xgots[l].at[bits[l]], x_s.at[l], x_r.at[l], (pole, mates[l]))
        xgots[l][bits[l]] = jnp.where(is_low, x_left, x_right)
        copy.wait_recv()
        x_copies.append(copy)
        x = xgots[l][...].reshape(-1, 4 * s)

    rows = ni // poles
    for q in range(poles):
        part[q] = first[q * rows : (q + 1) * rows] + dot(maps[q * rows : (q + 1) * rows], x, 1, 1)
    o_copies = [
        send(part.at[peer], got.at[o], o_s.at[o], o_r.at[o], (peer, dom)) for o, peer in enumerate(peers)
    ]
    weighted_sep = jnp.transpose(wr * x[:, : 2 * s] - wi * x[:, 2 * s :])[s:]
    rows_sep = s // poles
    for q in range(poles):
        part_sep[q] = weighted_sep[q * rows_sep : (q + 1) * rows_sep]
    p_copies = [
        send(part_sep.at[peer], got_sep.at[o], p_s.at[o], p_r.at[o], (peer, dom))
        for o, peer in enumerate(peers)
    ]
    total = part[pole]
    for o in range(len(peers)):
        o_copies[o].wait_recv()
        total = total + got[o]
    out_ref[...] = total
    total = part_sep[pole]
    for o in range(len(peers)):
        p_copies[o].wait_recv()
        total = total + got_sep[o]
    outsep_ref[...] = total
    for copy in y_copies + s_copies + t_copies + x_copies + o_copies + p_copies:
        copy.wait_send()


def shards(poles, doms, y_interior, y_separator, green, pole_data, coupling, sep_block, iface_rows):
    rows, m = y_interior.shape[1:]
    s = sep_block.shape[-1]
    ni = green.shape[-1]
    levels = doms.bit_length() - 1
    others = max(poles - 1, 1)
    vmem = pl.BlockSpec(memory_space=pltpu.VMEM)
    dma = pltpu.SemaphoreType.DMA
    buf = lambda *shape: pltpu.VMEM(shape, f32)
    widths = [m >> (l + 1) for l in range(levels)]
    out, out_sep = pl.pallas_call(
        functools.partial(kernel, poles, doms),
        out_shape=(
            jax.ShapeDtypeStruct((rows, m), f32),
            jax.ShapeDtypeStruct((s // poles, m), f32),
        ),
        in_specs=[vmem, vmem, vmem, pl.BlockSpec(memory_space=pltpu.SMEM), vmem, vmem, vmem],
        out_specs=(vmem, vmem),
        scratch_shapes=[
            buf(poles, rows, m),
            buf(poles, rows, m),
            buf(poles, s // poles, m),
            buf(others, rows, m),
            buf(others, s // poles, m),
            buf(levels, 2 * s, 4 * s),
            buf(levels, 2 * s, 4 * s),
            [buf(2, w, 4 * s) for w in widths],
            [buf(w, 4 * s) for w in widths],
            [buf(w, 4 * s) for w in widths],
            [buf(2, w, 4 * s) for w in widths],
            buf(ni, m),
            buf(ni, 4 * s),
            dma((others,)), dma((others,)),
            dma((levels,)), dma((levels,)),
            dma((levels,)), dma((levels,)),
            dma((levels,)), dma((levels,)),
            dma((others,)), dma((others,)),
            dma((others,)), dma((others,)),
        ],
        compiler_params=pltpu.CompilerParams(
            collective_id=0, has_side_effects=True, vmem_limit_bytes=40 * 1024 * 1024
        ),
    )(
        y_interior[0], y_separator[0], green[:, 0, 0], pole_data[:, 0], coupling[0], sep_block[0],
        iface_rows[0][:, :, None],
    )
    return out[None], out_sep[None]


def solution(mesh):
    return jax.shard_map(
        functools.partial(shards, mesh.shape["pole"], mesh.shape["dom"]),
        mesh=mesh,
        in_specs=(
            P("dom", "pole", None),
            P("dom", None, None),
            P(None, "pole", "dom", None, None),
            P(None, "pole"),
            P("dom", None, None, None),
            P("dom", None, None),
            P("dom", None, None),
        ),
        out_specs=(P("dom", "pole", None), P("dom", "pole", None)),
        check_vma=False,
    )
```

```python
import functools
import jax
import jax.numpy as jnp
from jax import lax
from jax.experimental import pallas as pl
from jax.experimental.pallas import tpu as pltpu
from jax.sharding import PartitionSpec as P

MESH = pl.DeviceIdType.MESH
f32 = jnp.float32


def split(value):
    high = value.astype(jnp.bfloat16)
    return high, (value - high.astype(f32)).astype(jnp.bfloat16)


def dot(a, b, ca=1, cb=0):
    a_high, a_low = a if isinstance(a, tuple) else split(a)
    b_high, b_low = b if isinstance(b, tuple) else split(b)

    def one(u, v):
        return lax.dot_general(u, v, (((ca,), (cb,)), ((), ())), preferred_element_type=f32)

    return one(a_high, b_high) + (one(a_high, b_low) + one(a_low, b_high))


def lanes_below(shape, limit):
    return lax.broadcasted_iota(jnp.int32, shape, 1) < limit


def swap(value, half):
    return pltpu.roll(value, half, 1)


def small_inverse(dr, di):
    n = len(dr)
    row = lax.broadcasted_iota(jnp.int32, dr[0].shape, 0)
    for k in range(n):
        pr, pi = dr[k][k : k + 1], di[k][k : k + 1]
        scale = 1.0 / (pr * pr + pi * pi)
        qr, qi = pr * scale, -pi * scale
        here = row == k
        cr, ci = dr[k], di[k]
        new_r, new_i = [], []
        for m in range(n):
            if m == k:
                new_r.append(jnp.where(here, qr, ci * qi - cr * qr))
                new_i.append(jnp.where(here, qi, -(cr * qi + ci * qr)))
            else:
                tr, ti = dr[m][k : k + 1], di[m][k : k + 1]
                rr, ri = tr * qr - ti * qi, tr * qi + ti * qr
                new_r.append(jnp.where(here, rr, dr[m] - cr * rr + ci * ri))
                new_i.append(jnp.where(here, ri, di[m] - cr * ri - ci * rr))
        dr, di = new_r, new_i
    return dr, di


def inverse(packed):
    n = packed.shape[0]
    step, steps = 8, 4
    lane = lax.broadcasted_iota(jnp.int32, packed.shape, 1)
    within = lax.rem(lane, n)
    sign = jnp.where(lane[:step] < n, -1.0, 1.0)
    row = lax.broadcasted_iota(jnp.int32, (step, 2 * n), 0)

    def body(_, a):
        shape = a.shape
        for b in range(steps):
            at = b * step
            swept = (within >= at) & (within < at + step)
            unit = (lane[:step] == row + at).astype(f32)
            col_r = [jnp.broadcast_to(a[:, at + m : at + m + 1], shape) for m in range(step)]
            col_i = [jnp.broadcast_to(a[:, n + at + m : n + at + m + 1], shape) for m in range(step)]
            inv_r, inv_i = small_inverse(
                [c[at : at + step] for c in col_r], [c[at : at + step] for c in col_i]
            )
            top = jnp.where(swept[:step], unit, a[at : at + step])
            turned = swap(top, n) * sign
            r = jnp.zeros_like(top)
            ri = jnp.zeros_like(top)
            for m in range(step):
                tm, um = top[m : m + 1], turned[m : m + 1]
                r = r + inv_r[m] * tm + inv_i[m] * um
                ri = ri + inv_r[m] * um - inv_i[m] * tm
            rest = jnp.where(swept, 0.0, a)
            for m in range(step):
                rest = rest - col_r[m] * r[m : m + 1] - col_i[m] * ri[m : m + 1]
            pieces = [rest[:at], r, rest[at + step :]] if at else [r, rest[step:]]
            a = jnp.concatenate(pieces, axis=0)
        move = step * steps
        a = jnp.concatenate([a[move:], a[:move]], axis=0)
        return jnp.where(within < n - move, pltpu.roll(a, 2 * n - move, 1), pltpu.roll(a, n - move, 1))

    return lax.fori_loop(0, n // (step * steps), body, packed)


def embed(re, im):
    return jnp.concatenate(
        [jnp.concatenate([re, im], axis=1), jnp.concatenate([-im, re], axis=1)], axis=0
    )


def embed_packed(packed):
    n = packed.shape[1] // 2
    turned = swap(packed, n) * jnp.where(lanes_below(packed.shape, n), -1.0, 1.0)
    return jnp.concatenate([packed, turned], axis=0)


def kernel(
    poles, doms, y_hbm, ysep_hbm, green_hbm, pole_ref, coup_hbm, sep_hbm, rows_hbm,
    out_ref, outsep_ref,
    ysep_ref, green_ref, coup_ref, sep_ref, rows_ref,
    ybuf, part, part_sep, got, got_sep, sbuf, sgot, ebuf, egot, tbufs, tgots, xsends, xgots, first, maps,
    load, y_s, y_r, s_s, s_r, t_s, t_r, x_s, x_r, o_s, o_r, p_s, p_r,
):
    levels = doms.bit_length() - 1
    top = levels - 1
    pole = lax.axis_index("pole")
    dom = lax.axis_index("dom")
    bits = [lax.rem(lax.div(dom, 1 << l), 2) for l in range(levels)]
    mates = [dom + (1 - 2 * bits[l]) * (1 << l) for l in range(levels)]
    peers = [lax.rem(pole + o, poles) for o in range(1, poles)]

    def fetch(src, dst, number):
        copy = pltpu.make_async_copy(src, dst, load.at[number])
        copy.start()
        return copy

    def send(src, dst, send_sem, recv_sem, place):
        copy = pltpu.make_async_remote_copy(
            src_ref=src, dst_ref=dst, send_sem=send_sem, recv_sem=recv_sem,
            device_id=place, device_id_type=MESH,
        )
        copy.start()
        return copy

    loads = [
        fetch(rows_hbm, rows_ref, 0),
        fetch(coup_hbm, coup_ref, 1),
        fetch(green_hbm, green_ref, 2),
        fetch(sep_hbm, sep_ref, 3),
        fetch(y_hbm, ybuf.at[pole], 4),
        fetch(ysep_hbm, ysep_ref, 5),
    ]
    barrier = pltpu.get_barrier_semaphore()
    for peer in peers:
        pl.semaphore_signal(barrier, inc=1, device_id=(peer, dom), device_id_type=MESH)
    for mate in mates:
        pl.semaphore_signal(barrier, inc=1, device_id=(pole, mate), device_id_type=MESH)
    pl.semaphore_wait(barrier, len(peers) + len(mates))
    y_copies = [
        send(y_hbm, ybuf.at[pole], y_s.at[o], y_r.at[o], (peer, dom)) for o, peer in enumerate(peers)
    ]

    s = sep_ref.shape[0]
    ni = green_ref.shape[1]
    m = y_hbm.shape[1]
    zr, zi, wr, wi = pole_ref[0, 0], pole_ref[1, 0], pole_ref[2, 0], pole_ref[3, 0]
    for copy in loads[:2]:
        copy.wait()
    spot = lax.broadcasted_iota(jnp.int32, (ni, rows_ref.shape[1]), 0)
    pick_u = (spot == rows_ref[0:1]).astype(f32)
    pick_w = (spot == rows_ref[1:2]).astype(f32)
    has_left = (dom > 0).astype(f32)
    c = split(
        jnp.concatenate([dot(coup_ref[1] * has_left, pick_w, 1, 1), dot(coup_ref[0], pick_u, 1, 1)], axis=0)
    )
    for copy in loads[2:4]:
        copy.wait()
    n_r = dot(c, green_ref[0])
    n_i = dot(c, green_ref[1])
    n_rs, n_is = split(n_r), split(n_i)
    k_r = dot(n_rs, c, 1, 1)
    k_i = dot(n_is, c, 1, 1)
    eye = (
        lax.broadcasted_iota(jnp.int32, (s, s), 0) == lax.broadcasted_iota(jnp.int32, (s, s), 1)
    ).astype(f32)
    gap = jnp.zeros((s, s), f32)

    def place_corner(block):
        under = jnp.concatenate([gap, block], axis=1)
        return jnp.concatenate([jnp.zeros_like(under), under], axis=0)

    corner_r, corner_i = zr * eye - sep_ref[...], zi * eye
    merged = jnp.concatenate([place_corner(corner_r) - k_r, place_corner(corner_i) - k_i], axis=1)
    low = lanes_below((s, 2 * s), s)
    kept = []
    s_copies, t_copies, x_copies = [], [], []

    def send_matrix(l):
        sbuf[l] = merged
        s_copies.append(send(sbuf.at[l], sgot.at[l], s_s.at[l], s_r.at[l], (pole, mates[l])))

    def send_rights(l, t):
        width = t.shape[0] // 2
        tbufs[l][0] = t[:width]
        tbufs[l][1] = t[width:]
        t_copies.append(
            send(tbufs[l].at[1 - bits[l]], tgots[l], t_s.at[l], t_r.at[l], (pole, mates[l]))
        )

    if top:
        send_matrix(0)
    maps[:, : 2 * s] = jnp.transpose(wr * n_r - wi * n_i)
    maps[:, 2 * s :] = jnp.transpose(-(wr * n_i + wi * n_r))
    halves = 2
    wide = m // halves

    def start_rights():
        for copy in loads[4:]:
            copy.wait()
        for copy in y_copies:
            copy.wait_recv()
        y_all = split(ybuf[...].reshape(ni, m))
        right_r = jnp.transpose(dot(n_rs, y_all))
        right_i = jnp.transpose(dot(n_is, y_all))
        sep_t = jnp.transpose(jnp.concatenate([jnp.zeros((s, m), f32), ysep_ref[...]], axis=0))
        return jnp.concatenate([right_r + sep_t, right_i], axis=1), y_all

    def merge_rights(l, z_emb, pinv_emb, back):
        t_copies[l].wait_recv()
        width = tgots[l].shape[0]
        is_low = bits[l] == 0
        t_mine, t_other = tbufs[l][bits[l]], tgots[l][...]
        t_left = jnp.where(is_low, t_mine, t_other)
        t_right = jnp.where(is_low, t_other, t_mine)
        below = lanes_below((width, 2 * s), s)
        sum_r = swap(t_left[:, : 2 * s], s) + t_right[:, : 2 * s]
        sum_i = swap(t_left[:, 2 * s :], s) + t_right[:, 2 * s :]
        middle = split(jnp.where(below, sum_r, swap(sum_i, s)))
        ends = jnp.concatenate(
            [
                jnp.where(below, t_left[:, : 2 * s], t_right[:, : 2 * s]),
                jnp.where(below, t_left[:, 2 * s :], t_right[:, 2 * s :]),
            ],
            axis=1,
        )
        kept.append((dot(middle, pinv_emb), back, below))
        return ends - dot(middle, z_emb)

    y_all = None
    t = None
    for l in range(top):
        is_low = bits[l] == 0
        s_copies[l].wait_recv()
        mine, other = sbuf[l], sgot[l]
        left = jnp.where(is_low, mine, other)
        right = jnp.where(is_low, other, mine)
        lr, li = left[:, : 2 * s], left[:, 2 * s :]
        rr, ri = right[:, : 2 * s], right[:, 2 * s :]
        pivot = jnp.where(low, swap(lr[s:], s) + rr[:s], swap(swap(li[s:], s) + ri[:s], s))
        y_re = jnp.where(low, lr[s:], rr[:s])
        y_im = jnp.where(low, li[s:], ri[:s])
        turned = split(jnp.transpose(jnp.concatenate([y_re, y_im], axis=0)))
        y_emb = split(embed(y_re, y_im))
        base = jnp.concatenate(
            [
                jnp.concatenate([jnp.where(low, lr[:s], 0.0), jnp.where(low, li[:s], 0.0)], axis=1),
                jnp.concatenate([jnp.where(low, 0.0, rr[s:]), jnp.where(low, 0.0, ri[s:])], axis=1),
            ],
            axis=0,
        )
        pinv = inverse(pivot)
        z = dot(pinv, y_emb)
        z_re, z_im = z[:, : 2 * s], z[:, 2 * s :]
        z_emb = split(embed(z_re, z_im))
        merged = base - dot(turned, z_emb)
        back = split(
            jnp.concatenate(
                [jnp.concatenate([z_re, -z_im], axis=1), jnp.concatenate([z_im, z_re], axis=1)], axis=0
            )
        )
        if l + 1 < top:
            send_matrix(l + 1)
        if l == 0:
            t, y_all = start_rights()
            send_rights(0, t)
            if l + 1 < top:
                weighted = wr * green_ref[0] - wi * green_ref[1]
                first[...] = dot(weighted, y_all)
        if l + 1 < top:
            t = merge_rights(l, z_emb, embed_packed(pinv), back)
            send_rights(l + 1, t)
        last = (z_emb, pinv, back)
    if not top:
        t, y_all = start_rights()
    if top < 2:
        weighted = wr * green_ref[0] - wi * green_ref[1]
        first[...] = dot(weighted, y_all)

    upper = bits[top] == 1
    end_pivot = jnp.where(low, swap(merged[s:, : 2 * s], s), merged[s:, 2 * s :])
    end_row = jnp.where(low, merged[s:, : 2 * s], swap(merged[s:, 2 * s :], s))
    end_col = jnp.where(low, swap(merged[:s, : 2 * s], s), merged[:s, 2 * s :])
    near = jnp.where(low, merged[:s, : 2 * s], swap(merged[:s, 2 * s :], s))
    row_emb = split(embed_packed(end_row))
    end_inv = inverse(end_pivot)
    end_z = dot(end_inv, row_emb)
    end_emb = split(embed_packed(end_z))
    ebuf[...] = jnp.where(upper, near - dot(end_col, end_emb), end_pivot)
    s_copies.append(send(ebuf, egot, s_s.at[top], s_r.at[top], (pole, mates[top])))
    if top:
        z_emb, pinv, back = last
        t = merge_rights(top - 1, z_emb, embed_packed(pinv), back)
    width = t.shape[0]
    below = lanes_below((width, 2 * s), s)
    t_end = jnp.where(below, swap(t[:, : 2 * s], s), t[:, 2 * s :])
    t_near = jnp.where(below, t[:, : 2 * s], swap(t[:, 2 * s :], s))
    t_ends = split(t_end)
    send_rights(top, jnp.where(upper, t_near - dot(t_ends, end_emb), t_end))
    x_part = dot(t_ends, embed_packed(end_inv))
    end_back = split(jnp.concatenate([jnp.where(low, end_z, -end_z), swap(end_z, s)], axis=0))
    s_copies[top].wait_recv()
    middle_inv = split(embed_packed(inverse(ebuf[...] + egot[...])))
    t_copies[top].wait_recv()
    xsends[top][...] = dot(tbufs[top][bits[top]] + tgots[top][...], middle_inv)

    def trade(l):
        copy = send(xsends[l], xgots[l].at[bits[l]], x_s.at[l], x_r.at[l], (pole, mates[l]))
        x_copies.append(copy)
        return copy

    copy = trade(top)
    xgots[top][bits[top]] = xsends[top][...]
    copy.wait_recv()
    xm = xgots[top][...].reshape(width, 2 * s)
    xm_t = swap(xm, s)
    x_end = x_part - dot(xm, end_back, 1, 1)
    x_end_t = swap(x_end, s)
    zero = jnp.zeros_like(xm)
    x = jnp.where(
        upper,
        jnp.concatenate([jnp.where(below, xm, x_end_t), jnp.where(below, xm_t, x_end)], axis=1),
        jnp.concatenate([jnp.where(below, zero, xm_t), jnp.where(below, zero, xm)], axis=1),
    )
    for l in reversed(range(top)):
        part_m, back, below = kept[l]
        xm = part_m - dot(x, back, 1, 1)
        xr, xi = x[:, : 2 * s], x[:, 2 * s :]
        xm_t = swap(xm, s)
        x_left = jnp.concatenate([jnp.where(below, xr, xm_t), jnp.where(below, xi, xm)], axis=1)
        x_right = jnp.concatenate([jnp.where(below, xm, xr), jnp.where(below, xm_t, xi)], axis=1)
        is_low = bits[l] == 0
        xsends[l][...] = jnp.where(is_low, x_right, x_left)
        copy = trade(l)
        xgots[l][bits[l]] = jnp.where(is_low, x_left, x_right)
        if l:
            copy.wait_recv()
            x = xgots[l][...].reshape(-1, 4 * s)
    if not top:
        xgots[0 if top else 1][...] = x.reshape(2, wide, 4 * s)

    rows = ni // poles
    rows_sep = s // poles
    o_copies, p_copies = [], []
    for turn in range(halves):
        half = bits[0] if turn == 0 else 1 - bits[0]
        columns = pl.ds(pl.multiple_of(half * wide, wide), wide)
        if turn and top:
            copy.wait_recv()
        xh = xgots[0 if top else 1][half]
        xhs = split(xh)
        for o, peer in enumerate(peers + [pole]):
            at = pl.ds(pl.multiple_of(peer * rows, rows), rows)
            part[turn, peer] = first[at, columns] + dot(maps[at, :], xhs, 1, 1)
            if o < len(peers):
                o_copies.append(
                    send(
                        part.at[turn, peer], got.at[o, :, columns],
                        o_s.at[turn, o], o_r.at[turn, o], (peer, dom),
                    )
                )
        weighted_sep = jnp.transpose(wr * xh[:, : 2 * s] - wi * xh[:, 2 * s :])[s:]
        for q in range(poles):
            part_sep[q, :, columns] = weighted_sep[q * rows_sep : (q + 1) * rows_sep]
    for o, peer in enumerate(peers):
        p_copies.append(
            send(part_sep.at[peer], got_sep.at[o], p_s.at[o], p_r.at[o], (peer, dom))
        )
    for turn in range(halves):
        half = bits[0] if turn == 0 else 1 - bits[0]
        columns = pl.ds(pl.multiple_of(half * wide, wide), wide)
        out_ref[:, columns] = part[turn, pole]
    for copy in o_copies:
        copy.wait_recv()
    total = out_ref[...]
    for o in range(len(peers)):
        total = total + got[o]
    out_ref[...] = total
    total = part_sep[pole]
    for o in range(len(peers)):
        p_copies[o].wait_recv()
        total = total + got_sep[o]
    outsep_ref[...] = total
    for copy in y_copies + s_copies + t_copies + x_copies + o_copies + p_copies:
        copy.wait_send()


def shards(poles, doms, y_interior, y_separator, green, pole_data, coupling, sep_block, iface_rows):
    rows, m = y_interior.shape[1:]
    s = sep_block.shape[-1]
    ni = green.shape[-1]
    levels = doms.bit_length() - 1
    others = max(poles - 1, 1)
    b = iface_rows.shape[-1]
    vmem = pl.BlockSpec(memory_space=pltpu.VMEM)
    hbm = pl.BlockSpec(memory_space=pl.ANY)
    dma = pltpu.SemaphoreType.DMA
    buf = lambda *shape: pltpu.VMEM(shape, f32)
    widths = [m >> (l + 1) for l in range(levels)]
    cols = [4 * s] * (levels - 1) + [2 * s]
    sizes = list(zip(widths, cols))
    out, out_sep = pl.pallas_call(
        functools.partial(kernel, poles, doms),
        out_shape=(
            jax.ShapeDtypeStruct((rows, m), f32),
            jax.ShapeDtypeStruct((s // poles, m), f32),
        ),
        in_specs=[hbm, hbm, hbm, pl.BlockSpec(memory_space=pltpu.SMEM), hbm, hbm, hbm],
        out_specs=(vmem, vmem),
        scratch_shapes=[
            buf(s, m),
            buf(2, ni, ni),
            buf(2, s, b),
            buf(s, s),
            pltpu.VMEM((2, b), jnp.int32),
            buf(poles, rows, m),
            buf(2, poles, rows, m // 2),
            buf(poles, s // poles, m),
            buf(others, rows, m),
            buf(others, s // poles, m),
            buf(max(levels - 1, 1), 2 * s, 4 * s),
            buf(max(levels - 1, 1), 2 * s, 4 * s),
            buf(s, 2 * s),
            buf(s, 2 * s),
            [buf(2, w, c) for w, c in sizes],
            [buf(w, c) for w, c in sizes],
            [buf(w, c) for w, c in sizes],
            [buf(2, w, c) for w, c in sizes] + [buf(2, m // 2, 4 * s)],
            buf(ni, m),
            buf(ni, 4 * s),
            dma((6,)),
            dma((others,)), dma((others,)),
            dma((levels,)), dma((levels,)),
            dma((levels,)), dma((levels,)),
            dma((levels,)), dma((levels,)),
            dma((2, others)), dma((2, others)),
            dma((others,)), dma((others,)),
        ],
        compiler_params=pltpu.CompilerParams(
            collective_id=0, has_side_effects=True, vmem_limit_bytes=56 * 1024 * 1024
        ),
    )(
        y_interior[0], y_separator[0], green[:, 0, 0], pole_data, coupling[0], sep_block[0],
        iface_rows[0],
    )
    return out[None], out_sep[None]


def solution(mesh):
    return jax.shard_map(
        functools.partial(shards, mesh.shape["pole"], mesh.shape["dom"]),
        mesh=mesh,
        in_specs=(
            P("dom", "pole", None),
            P("dom", None, None),
            P(None, "pole", "dom", None, None),
            P(None, "pole"),
            P("dom", None, None, None),
            P("dom", None, None),
            P("dom", None, None),
        ),
        out_specs=(P("dom", "pole", None), P("dom", "pole", None)),
        check_vma=False,
    )
```

```python
import functools
import jax
import jax.numpy as jnp
from jax import lax
from jax.experimental import pallas as pl
from jax.experimental.pallas import tpu as pltpu
from jax.sharding import PartitionSpec as P

MESH = pl.DeviceIdType.MESH
f32 = jnp.float32


def split(value):
    high = value.astype(jnp.bfloat16)
    return high, (value - high.astype(f32)).astype(jnp.bfloat16)


def dot(a, b, ca=1, cb=0):
    a_high, a_low = a if isinstance(a, tuple) else split(a)
    b_high, b_low = b if isinstance(b, tuple) else split(b)

    def one(u, v):
        return lax.dot_general(u, v, (((ca,), (cb,)), ((), ())), preferred_element_type=f32)

    return one(a_high, b_high) + (one(a_high, b_low) + one(a_low, b_high))


def lanes_below(shape, limit):
    return lax.broadcasted_iota(jnp.int32, shape, 1) < limit


def swap(value, half):
    return pltpu.roll(value, half, 1)


def sweep_rows(dr, di, top, turned):
    n = len(dr)
    row = lax.broadcasted_iota(jnp.int32, top.shape, 0)
    for k in range(n):
        pr, pi = dr[k][k : k + 1], di[k][k : k + 1]
        scale = 1.0 / (pr * pr + pi * pi)
        qr, qi = pr * scale, -pi * scale
        here = row == k
        cr, ci = dr[k], di[k]

        def reduced(re, im):
            tr, ti = re[k : k + 1], im[k : k + 1]
            rr, ri = tr * qr - ti * qi, tr * qi + ti * qr
            return (
                jnp.where(here, rr, re - cr * rr + ci * ri),
                jnp.where(here, ri, im - cr * ri - ci * rr),
            )

        later = [reduced(dr[m], di[m]) for m in range(k + 1, n)]
        dr = dr[: k + 1] + [pair[0] for pair in later]
        di = di[: k + 1] + [pair[1] for pair in later]
        top, turned = reduced(top, turned)
    return top, turned


def inverse(packed):
    n = packed.shape[0]
    step, steps = 8, 4
    lane = lax.broadcasted_iota(jnp.int32, packed.shape, 1)
    within = lax.rem(lane, n)
    sign = jnp.where(lane[:step] < n, 1.0, -1.0)
    row = lax.broadcasted_iota(jnp.int32, (step, 2 * n), 0)

    def body(_, a):
        shape = a.shape
        for b in range(steps):
            at = b * step
            swept = (within >= at) & (within < at + step)
            unit = (lane[:step] == row + at).astype(f32)
            col_r = [jnp.broadcast_to(a[:, at + m : at + m + 1], shape) for m in range(step)]
            col_i = [jnp.broadcast_to(a[:, n + at + m : n + at + m + 1], shape) for m in range(step)]
            top = jnp.where(swept[:step], unit, a[at : at + step])
            turned = swap(top, n) * sign
            r, ri = sweep_rows(
                [c[at : at + step] for c in col_r], [c[at : at + step] for c in col_i], top, turned
            )
            rest = jnp.where(swept, 0.0, a)
            for m in range(step):
                rest = rest - col_r[m] * r[m : m + 1] + col_i[m] * ri[m : m + 1]
            pieces = [rest[:at], r, rest[at + step :]] if at else [r, rest[step:]]
            a = jnp.concatenate(pieces, axis=0)
        move = step * steps
        a = jnp.concatenate([a[move:], a[:move]], axis=0)
        return jnp.where(within < n - move, pltpu.roll(a, 2 * n - move, 1), pltpu.roll(a, n - move, 1))

    return lax.fori_loop(0, n // (step * steps), body, packed)


def embed(re, im):
    return jnp.concatenate(
        [jnp.concatenate([re, im], axis=1), jnp.concatenate([-im, re], axis=1)], axis=0
    )


def embed_packed(packed):
    n = packed.shape[1] // 2
    turned = swap(packed, n) * jnp.where(lanes_below(packed.shape, n), -1.0, 1.0)
    return jnp.concatenate([packed, turned], axis=0)


def kernel(
    poles, doms, y_hbm, ysep_hbm, green_hbm, pole_ref, coup_hbm, sep_hbm, rows_hbm,
    got, got_sep,
    ysep_ref, green_ref, coup_ref, sep_ref, rows_ref,
    ybuf, part, part_sep, sbuf, sgot, ebuf, egot, tbufs, tgots, xsends, xgots, first, maps,
    load, y_s, y_r, s_s, s_r, t_s, t_r, x_s, x_r, o_s, o_r, p_s, p_r,
):
    levels = doms.bit_length() - 1
    top = levels - 1
    pole = lax.axis_index("pole")
    dom = lax.axis_index("dom")
    bits = [lax.rem(lax.div(dom, 1 << l), 2) for l in range(levels)]
    mates = [dom + (1 - 2 * bits[l]) * (1 << l) for l in range(levels)]
    peers = [lax.rem(pole + o, poles) for o in range(1, poles)]

    def fetch(src, dst, number):
        copy = pltpu.make_async_copy(src, dst, load.at[number])
        copy.start()
        return copy

    def send(src, dst, send_sem, recv_sem, place):
        copy = pltpu.make_async_remote_copy(
            src_ref=src, dst_ref=dst, send_sem=send_sem, recv_sem=recv_sem,
            device_id=place, device_id_type=MESH,
        )
        copy.start()
        return copy

    loads = [
        fetch(rows_hbm, rows_ref, 0),
        fetch(coup_hbm, coup_ref, 1),
        fetch(green_hbm, green_ref, 2),
        fetch(sep_hbm, sep_ref, 3),
        fetch(y_hbm, ybuf.at[pole], 4),
        fetch(ysep_hbm, ysep_ref, 5),
    ]
    barrier = pltpu.get_barrier_semaphore()
    for peer in peers:
        pl.semaphore_signal(barrier, inc=1, device_id=(peer, dom), device_id_type=MESH)
    for mate in mates:
        pl.semaphore_signal(barrier, inc=1, device_id=(pole, mate), device_id_type=MESH)

    s = sep_ref.shape[0]
    ni = green_ref.shape[1]
    m = y_hbm.shape[1]
    zr, zi, wr, wi = pole_ref[0], pole_ref[1], pole_ref[2], pole_ref[3]
    for copy in loads[:2]:
        copy.wait()
    spot = lax.broadcasted_iota(jnp.int32, (ni, rows_ref.shape[1]), 0)
    pick_u = (spot == rows_ref[0:1]).astype(f32)
    pick_w = (spot == rows_ref[1:2]).astype(f32)
    has_left = (dom > 0).astype(f32)
    c = split(
        jnp.concatenate([dot(coup_ref[1] * has_left, pick_w, 1, 1), dot(coup_ref[0], pick_u, 1, 1)], axis=0)
    )
    for copy in loads[2:4]:
        copy.wait()
    n_r = dot(c, green_ref[0])
    n_i = dot(c, green_ref[1])
    n_rs, n_is = split(n_r), split(n_i)
    pl.semaphore_wait(barrier, len(peers) + len(mates))
    y_copies = [
        send(y_hbm, ybuf.at[pole], y_s.at[o], y_r.at[o], (peer, dom)) for o, peer in enumerate(peers)
    ]
    k_r = dot(n_rs, c, 1, 1)
    k_i = dot(n_is, c, 1, 1)
    eye = (
        lax.broadcasted_iota(jnp.int32, (s, s), 0) == lax.broadcasted_iota(jnp.int32, (s, s), 1)
    ).astype(f32)
    gap = jnp.zeros((s, s), f32)

    def place_corner(block):
        under = jnp.concatenate([gap, block], axis=1)
        return jnp.concatenate([jnp.zeros_like(under), under], axis=0)

    corner_r, corner_i = zr * eye - sep_ref[...], zi * eye
    merged = jnp.concatenate([place_corner(corner_r) - k_r, place_corner(corner_i) - k_i], axis=1)
    low = lanes_below((s, 2 * s), s)
    kept = []
    s_copies, t_copies, x_copies = [], [], []

    def send_matrix(l):
        sbuf[l] = merged
        s_copies.append(send(sbuf.at[l], sgot.at[l], s_s.at[l], s_r.at[l], (pole, mates[l])))

    def send_rights(l, t):
        width = t.shape[0] // 2
        tbufs[l][0] = t[:width]
        tbufs[l][1] = t[width:]
        t_copies.append(
            send(tbufs[l].at[1 - bits[l]], tgots[l], t_s.at[l], t_r.at[l], (pole, mates[l]))
        )

    if top:
        send_matrix(0)
    maps[:, : 2 * s] = jnp.transpose(wr * n_r - wi * n_i)
    maps[:, 2 * s :] = jnp.transpose(-(wr * n_i + wi * n_r))
    halves = 2
    wide = m // halves

    def start_rights():
        for copy in loads[4:]:
            copy.wait()
        for copy in y_copies:
            copy.wait_recv()
        y_all = split(ybuf[...].reshape(ni, m))
        right_r = jnp.transpose(dot(n_rs, y_all))
        right_i = jnp.transpose(dot(n_is, y_all))
        sep_t = jnp.transpose(jnp.concatenate([jnp.zeros((s, m), f32), ysep_ref[...]], axis=0))
        return jnp.concatenate([right_r + sep_t, right_i], axis=1), y_all

    def merge_rights(l, z_emb, pinv_emb, back):
        t_copies[l].wait_recv()
        width = tgots[l].shape[0]
        is_low = bits[l] == 0
        t_mine, t_other = tbufs[l][bits[l]], tgots[l][...]
        t_left = jnp.where(is_low, t_mine, t_other)
        t_right = jnp.where(is_low, t_other, t_mine)
        below = lanes_below((width, 2 * s), s)
        sum_r = swap(t_left[:, : 2 * s], s) + t_right[:, : 2 * s]
        sum_i = swap(t_left[:, 2 * s :], s) + t_right[:, 2 * s :]
        middle = split(jnp.where(below, sum_r, swap(sum_i, s)))
        ends = jnp.concatenate(
            [
                jnp.where(below, t_left[:, : 2 * s], t_right[:, : 2 * s]),
                jnp.where(below, t_left[:, 2 * s :], t_right[:, 2 * s :]),
            ],
            axis=1,
        )
        kept.append((dot(middle, pinv_emb), back, below))
        return ends - dot(middle, z_emb)

    y_all = None
    t = None
    for l in range(top):
        is_low = bits[l] == 0
        s_copies[l].wait_recv()
        mine, other = sbuf[l], sgot[l]
        left = jnp.where(is_low, mine, other)
        right = jnp.where(is_low, other, mine)
        lr, li = left[:, : 2 * s], left[:, 2 * s :]
        rr, ri = right[:, : 2 * s], right[:, 2 * s :]
        pivot = jnp.where(low, swap(lr[s:], s) + rr[:s], swap(swap(li[s:], s) + ri[:s], s))
        y_re = jnp.where(low, lr[s:], rr[:s])
        y_im = jnp.where(low, li[s:], ri[:s])
        turned = split(jnp.transpose(jnp.concatenate([y_re, y_im], axis=0)))
        y_emb = split(embed(y_re, y_im))
        base = jnp.concatenate(
            [
                jnp.concatenate([jnp.where(low, lr[:s], 0.0), jnp.where(low, li[:s], 0.0)], axis=1),
                jnp.concatenate([jnp.where(low, 0.0, rr[s:]), jnp.where(low, 0.0, ri[s:])], axis=1),
            ],
            axis=0,
        )
        pinv = inverse(pivot)
        z = dot(pinv, y_emb)
        z_re, z_im = z[:, : 2 * s], z[:, 2 * s :]
        z_emb = split(embed(z_re, z_im))
        merged = base - dot(turned, z_emb)
        back = split(
            jnp.concatenate(
                [jnp.concatenate([z_re, -z_im], axis=1), jnp.concatenate([z_im, z_re], axis=1)], axis=0
            )
        )
        if l + 1 < top:
            send_matrix(l + 1)
        if l == 0:
            t, y_all = start_rights()
            send_rights(0, t)
            if l + 1 < top:
                weighted = wr * green_ref[0] - wi * green_ref[1]
                first[...] = dot(weighted, y_all)
        if l + 1 < top:
            t = merge_rights(l, z_emb, embed_packed(pinv), back)
            send_rights(l + 1, t)
        last = (z_emb, pinv, back)
    if not top:
        t, y_all = start_rights()
    if top < 2:
        weighted = wr * green_ref[0] - wi * green_ref[1]
        first[...] = dot(weighted, y_all)

    upper = bits[top] == 1
    end_pivot = jnp.where(low, swap(merged[s:, : 2 * s], s), merged[s:, 2 * s :])
    end_row = jnp.where(low, merged[s:, : 2 * s], swap(merged[s:, 2 * s :], s))
    end_col = jnp.where(low, swap(merged[:s, : 2 * s], s), merged[:s, 2 * s :])
    near = jnp.where(low, merged[:s, : 2 * s], swap(merged[:s, 2 * s :], s))
    row_emb = split(embed_packed(end_row))
    end_inv = inverse(end_pivot)
    end_z = dot(end_inv, row_emb)
    end_emb = split(embed_packed(end_z))
    ebuf[...] = jnp.where(upper, near - dot(end_col, end_emb), end_pivot)
    s_copies.append(send(ebuf, egot, s_s.at[top], s_r.at[top], (pole, mates[top])))
    if top:
        z_emb, pinv, back = last
        t = merge_rights(top - 1, z_emb, embed_packed(pinv), back)
    width = t.shape[0]
    below = lanes_below((width, 2 * s), s)
    t_end = jnp.where(below, swap(t[:, : 2 * s], s), t[:, 2 * s :])
    t_near = jnp.where(below, t[:, : 2 * s], swap(t[:, 2 * s :], s))
    t_ends = split(t_end)
    send_rights(top, jnp.where(upper, t_near - dot(t_ends, end_emb), t_end))
    x_part = dot(t_ends, embed_packed(end_inv))
    end_back = split(jnp.concatenate([jnp.where(low, end_z, -end_z), swap(end_z, s)], axis=0))
    s_copies[top].wait_recv()
    middle_inv = split(embed_packed(inverse(ebuf[...] + egot[...])))
    t_copies[top].wait_recv()
    xsends[top][...] = dot(tbufs[top][bits[top]] + tgots[top][...], middle_inv)

    def trade(l):
        copy = send(xsends[l], xgots[l].at[bits[l]], x_s.at[l], x_r.at[l], (pole, mates[l]))
        x_copies.append(copy)
        return copy

    copy = trade(top)
    xgots[top][bits[top]] = xsends[top][...]
    copy.wait_recv()
    xm = xgots[top][...].reshape(width, 2 * s)
    xm_t = swap(xm, s)
    x_end = x_part - dot(xm, end_back, 1, 1)
    x_end_t = swap(x_end, s)
    zero = jnp.zeros_like(xm)
    x = jnp.where(
        upper,
        jnp.concatenate([jnp.where(below, xm, x_end_t), jnp.where(below, xm_t, x_end)], axis=1),
        jnp.concatenate([jnp.where(below, zero, xm_t), jnp.where(below, zero, xm)], axis=1),
    )
    for l in reversed(range(top)):
        part_m, back, below = kept[l]
        xm = part_m - dot(x, back, 1, 1)
        xr, xi = x[:, : 2 * s], x[:, 2 * s :]
        xm_t = swap(xm, s)
        x_left = jnp.concatenate([jnp.where(below, xr, xm_t), jnp.where(below, xi, xm)], axis=1)
        x_right = jnp.concatenate([jnp.where(below, xm, xr), jnp.where(below, xm_t, xi)], axis=1)
        is_low = bits[l] == 0
        xsends[l][...] = jnp.where(is_low, x_right, x_left)
        copy = trade(l)
        xgots[l][bits[l]] = jnp.where(is_low, x_left, x_right)
        if l:
            copy.wait_recv()
            x = xgots[l][...].reshape(-1, 4 * s)
    if not top:
        xgots[0 if top else 1][...] = x.reshape(2, wide, 4 * s)

    rows = ni // poles
    rows_sep = s // poles
    o_copies, p_copies, own_copies = [], [], []
    for turn in range(halves):
        half = bits[0] if turn == 0 else 1 - bits[0]
        columns = pl.ds(pl.multiple_of(half * wide, wide), wide)
        if turn and top:
            copy.wait_recv()
        xh = xgots[0 if top else 1][half]
        xhs = split(xh)
        for o, peer in enumerate(peers + [pole]):
            at = pl.ds(pl.multiple_of(peer * rows, rows), rows)
            part[turn, peer] = first[at, columns] + dot(maps[at, :], xhs, 1, 1)
            if o == len(peers):
                own_copies.append(fetch(part.at[turn, peer], got.at[o, :, columns], 6 + turn))
            else:
                o_copies.append(
                    send(
                        part.at[turn, peer], got.at[o, :, columns],
                        o_s.at[turn, o], o_r.at[turn, o], (peer, dom),
                    )
                )
        weighted_sep = jnp.transpose(wr * xh[:, : 2 * s] - wi * xh[:, 2 * s :])[s:]
        for q in range(poles):
            part_sep[q, :, columns] = weighted_sep[q * rows_sep : (q + 1) * rows_sep]
    for o, peer in enumerate(peers):
        p_copies.append(
            send(part_sep.at[peer], got_sep.at[o], p_s.at[o], p_r.at[o], (peer, dom))
        )
    own_copies.append(fetch(part_sep.at[pole], got_sep.at[len(peers)], 8))
    for copy in o_copies + p_copies:
        copy.wait_recv()
    for copy in own_copies:
        copy.wait()
    for copy in y_copies + s_copies + t_copies + x_copies + o_copies + p_copies:
        copy.wait_send()


def shards(poles, doms, y_interior, y_separator, green, pole_data, coupling, sep_block, iface_rows):
    rows, m = y_interior.shape[1:]
    s = sep_block.shape[-1]
    ni = green.shape[-1]
    levels = doms.bit_length() - 1
    others = max(poles - 1, 1)
    b = iface_rows.shape[-1]
    hbm = pl.BlockSpec(memory_space=pl.ANY)
    dma = pltpu.SemaphoreType.DMA
    buf = lambda *shape: pltpu.VMEM(shape, f32)
    widths = [m >> (l + 1) for l in range(levels)]
    cols = [4 * s] * (levels - 1) + [2 * s]
    sizes = list(zip(widths, cols))
    out, out_sep = pl.pallas_call(
        functools.partial(kernel, poles, doms),
        out_shape=(
            jax.ShapeDtypeStruct((poles, rows, m), f32),
            jax.ShapeDtypeStruct((poles, s // poles, m), f32),
        ),
        in_specs=[hbm, hbm, hbm, pl.BlockSpec(memory_space=pltpu.SMEM), hbm, hbm, hbm],
        out_specs=(hbm, hbm),
        scratch_shapes=[
            buf(s, m),
            buf(2, ni, ni),
            buf(2, s, b),
            buf(s, s),
            pltpu.VMEM((2, b), jnp.int32),
            buf(poles, rows, m),
            buf(2, poles, rows, m // 2),
            buf(poles, s // poles, m),
            buf(max(levels - 1, 1), 2 * s, 4 * s),
            buf(max(levels - 1, 1), 2 * s, 4 * s),
            buf(s, 2 * s),
            buf(s, 2 * s),
            [buf(2, w, c) for w, c in sizes],
            [buf(w, c) for w, c in sizes],
            [buf(w, c) for w, c in sizes],
            [buf(2, w, c) for w, c in sizes] + [buf(2, m // 2, 4 * s)],
            buf(ni, m),
            buf(ni, 4 * s),
            dma((9,)),
            dma((others,)), dma((others,)),
            dma((levels,)), dma((levels,)),
            dma((levels,)), dma((levels,)),
            dma((levels,)), dma((levels,)),
            dma((2, others)), dma((2, others)),
            dma((others,)), dma((others,)),
        ],
        compiler_params=pltpu.CompilerParams(
            collective_id=0, has_side_effects=True, vmem_limit_bytes=56 * 1024 * 1024
        ),
    )(
        y_interior[0], y_separator[0], green[:, 0, 0], pole_data[:, 0], coupling[0], sep_block[0],
        iface_rows[0],
    )
    return jnp.sum(out, axis=0)[None], jnp.sum(out_sep, axis=0)[None]


def solution(mesh):
    return jax.shard_map(
        functools.partial(shards, mesh.shape["pole"], mesh.shape["dom"]),
        mesh=mesh,
        in_specs=(
            P("dom", "pole", None),
            P("dom", None, None),
            P(None, "pole", "dom", None, None),
            P(None, "pole"),
            P("dom", None, None, None),
            P("dom", None, None),
            P("dom", None, None),
        ),
        out_specs=(P("dom", "pole", None), P("dom", "pole", None)),
        check_vma=False,
    )
```

```python
import functools
import jax
import jax.numpy as jnp
from jax import lax
from jax.experimental import pallas as pl
from jax.experimental.pallas import tpu as pltpu
from jax.sharding import PartitionSpec as P

MESH = pl.DeviceIdType.MESH
f32 = jnp.float32


def split(value):
    high = value.astype(jnp.bfloat16)
    return high, (value - high.astype(f32)).astype(jnp.bfloat16)


def dot(a, b, ca=1, cb=0):
    a_high, a_low = a if isinstance(a, tuple) else split(a)
    b_high, b_low = b if isinstance(b, tuple) else split(b)

    def one(u, v):
        return lax.dot_general(u, v, (((ca,), (cb,)), ((), ())), preferred_element_type=f32)

    return one(a_high, b_high) + (one(a_high, b_low) + one(a_low, b_high))


def lanes_below(shape, limit):
    return lax.broadcasted_iota(jnp.int32, shape, 1) < limit


def swap(value, half):
    return pltpu.roll(value, half, 1)


def sweep_rows(dr, di, top, turned):
    n = len(dr)
    row = lax.broadcasted_iota(jnp.int32, top.shape, 0)
    for k in range(n):
        pr, pi = dr[k][k : k + 1], di[k][k : k + 1]
        scale = 1.0 / (pr * pr + pi * pi)
        qr, qi = pr * scale, -pi * scale
        here = row == k
        cr, ci = dr[k], di[k]

        def reduced(re, im):
            tr, ti = re[k : k + 1], im[k : k + 1]
            rr, ri = tr * qr - ti * qi, tr * qi + ti * qr
            return (
                jnp.where(here, rr, re - cr * rr + ci * ri),
                jnp.where(here, ri, im - cr * ri - ci * rr),
            )

        later = [reduced(dr[m], di[m]) for m in range(k + 1, n)]
        dr = dr[: k + 1] + [pair[0] for pair in later]
        di = di[: k + 1] + [pair[1] for pair in later]
        top, turned = reduced(top, turned)
    return top, turned


def inverse(packed):
    n = packed.shape[0]
    step, steps = 8, 4
    lane = lax.broadcasted_iota(jnp.int32, packed.shape, 1)
    within = lax.rem(lane, n)
    sign = jnp.where(lane[:step] < n, 1.0, -1.0)
    row = lax.broadcasted_iota(jnp.int32, (step, 2 * n), 0)

    def body(_, a):
        shape = a.shape
        for b in range(steps):
            at = b * step
            swept = (within >= at) & (within < at + step)
            unit = (lane[:step] == row + at).astype(f32)
            col_r = [jnp.broadcast_to(a[:, at + m : at + m + 1], shape) for m in range(step)]
            col_i = [jnp.broadcast_to(a[:, n + at + m : n + at + m + 1], shape) for m in range(step)]
            top = jnp.where(swept[:step], unit, a[at : at + step])
            turned = swap(top, n) * sign
            r, ri = sweep_rows(
                [c[at : at + step] for c in col_r], [c[at : at + step] for c in col_i], top, turned
            )
            rest = jnp.where(swept, 0.0, a)
            for m in range(step):
                rest = rest - col_r[m] * r[m : m + 1] + col_i[m] * ri[m : m + 1]
            pieces = [rest[:at], r, rest[at + step :]] if at else [r, rest[step:]]
            a = jnp.concatenate(pieces, axis=0)
        move = step * steps
        a = jnp.concatenate([a[move:], a[:move]], axis=0)
        return jnp.where(within < n - move, pltpu.roll(a, 2 * n - move, 1), pltpu.roll(a, n - move, 1))

    return lax.fori_loop(0, n // (step * steps), body, packed)


def embed(re, im):
    return jnp.concatenate(
        [jnp.concatenate([re, im], axis=1), jnp.concatenate([-im, re], axis=1)], axis=0
    )


def embed_packed(packed):
    n = packed.shape[1] // 2
    turned = swap(packed, n) * jnp.where(lanes_below(packed.shape, n), -1.0, 1.0)
    return jnp.concatenate([packed, turned], axis=0)


def kernel(
    poles, doms, y_hbm, ysep_hbm, green_hbm, pole_ref, coup_hbm, sep_hbm, rows_hbm,
    got, got_sep,
    ysep_ref, green_ref, coup_ref, sep_ref, rows_ref,
    ybuf, part, part_sep, sbuf, sgot, ebuf, egot, tbufs, tgots, xsends, xgots, first, maps,
    load, y_s, y_r, s_s, s_r, t_s, t_r, x_s, x_r, o_s, o_r, p_s, p_r,
):
    levels = doms.bit_length() - 1
    top = levels - 1
    pole = lax.axis_index("pole")
    dom = lax.axis_index("dom")
    bits = [lax.rem(lax.div(dom, 1 << l), 2) for l in range(levels)]
    mates = [dom + (1 - 2 * bits[l]) * (1 << l) for l in range(levels)]
    peers = [lax.rem(pole + o, poles) for o in range(1, poles)]

    def fetch(src, dst, number):
        copy = pltpu.make_async_copy(src, dst, load.at[number])
        copy.start()
        return copy

    def send(src, dst, send_sem, recv_sem, place):
        copy = pltpu.make_async_remote_copy(
            src_ref=src, dst_ref=dst, send_sem=send_sem, recv_sem=recv_sem,
            device_id=place, device_id_type=MESH,
        )
        copy.start()
        return copy

    loads = [
        fetch(rows_hbm, rows_ref, 0),
        fetch(coup_hbm, coup_ref, 1),
        fetch(green_hbm, green_ref, 2),
        fetch(sep_hbm, sep_ref, 3),
        fetch(y_hbm, ybuf.at[pole], 4),
        fetch(ysep_hbm, ysep_ref, 5),
    ]
    barrier = pltpu.get_barrier_semaphore()
    for peer in peers:
        pl.semaphore_signal(barrier, inc=1, device_id=(peer, dom), device_id_type=MESH)
    for mate in mates:
        pl.semaphore_signal(barrier, inc=1, device_id=(pole, mate), device_id_type=MESH)

    s = sep_ref.shape[0]
    ni = green_ref.shape[1]
    m = y_hbm.shape[1]
    zr, zi, wr, wi = pole_ref[0], pole_ref[1], pole_ref[2], pole_ref[3]
    for copy in loads[:2]:
        copy.wait()
    spot = lax.broadcasted_iota(jnp.int32, (ni, rows_ref.shape[1]), 0)
    pick_u = (spot == rows_ref[0:1]).astype(f32)
    pick_w = (spot == rows_ref[1:2]).astype(f32)
    has_left = (dom > 0).astype(f32)
    c = split(
        jnp.concatenate([dot(coup_ref[1] * has_left, pick_w, 1, 1), dot(coup_ref[0], pick_u, 1, 1)], axis=0)
    )
    for copy in loads[2:4]:
        copy.wait()
    n_r = dot(c, green_ref[0])
    n_i = dot(c, green_ref[1])
    n_rs, n_is = split(n_r), split(n_i)
    pl.semaphore_wait(barrier, len(peers) + len(mates))
    y_copies = [
        send(y_hbm, ybuf.at[pole], y_s.at[o], y_r.at[o], (peer, dom)) for o, peer in enumerate(peers)
    ]
    k_r = dot(n_rs, c, 1, 1)
    k_i = dot(n_is, c, 1, 1)
    eye = (
        lax.broadcasted_iota(jnp.int32, (s, s), 0) == lax.broadcasted_iota(jnp.int32, (s, s), 1)
    ).astype(f32)
    gap = jnp.zeros((s, s), f32)

    def place_corner(block):
        under = jnp.concatenate([gap, block], axis=1)
        return jnp.concatenate([jnp.zeros_like(under), under], axis=0)

    corner_r, corner_i = zr * eye - sep_ref[...], zi * eye
    merged = jnp.concatenate([place_corner(corner_r) - k_r, place_corner(corner_i) - k_i], axis=1)
    low = lanes_below((s, 2 * s), s)
    kept = []
    s_copies, t_copies, x_copies = [], [], []

    def send_matrix(l):
        sbuf[l] = merged
        s_copies.append(send(sbuf.at[l], sgot.at[l], s_s.at[l], s_r.at[l], (pole, mates[l])))

    def send_rights(l, t):
        width = t.shape[0] // 2
        tbufs[l][0] = t[:width]
        tbufs[l][1] = t[width:]
        t_copies.append(
            send(tbufs[l].at[1 - bits[l]], tgots[l], t_s.at[l], t_r.at[l], (pole, mates[l]))
        )

    if top:
        send_matrix(0)
    maps[:, : 2 * s] = jnp.transpose(wr * n_r - wi * n_i)
    maps[:, 2 * s :] = jnp.transpose(-(wr * n_i + wi * n_r))
    halves = 2
    wide = m // halves

    def start_rights():
        for copy in loads[4:]:
            copy.wait()
        for copy in y_copies:
            copy.wait_recv()
        y_all = split(ybuf[...].reshape(ni, m))
        right_r = jnp.transpose(dot(n_rs, y_all))
        right_i = jnp.transpose(dot(n_is, y_all))
        sep_t = jnp.transpose(jnp.concatenate([jnp.zeros((s, m), f32), ysep_ref[...]], axis=0))
        return jnp.concatenate([right_r + sep_t, right_i], axis=1), y_all

    def merge_rights(l, z_emb, pinv_emb, back):
        t_copies[l].wait_recv()
        width = tgots[l].shape[0]
        is_low = bits[l] == 0
        t_mine, t_other = tbufs[l][bits[l]], tgots[l][...]
        t_left = jnp.where(is_low, t_mine, t_other)
        t_right = jnp.where(is_low, t_other, t_mine)
        below = lanes_below((width, 2 * s), s)
        sum_r = swap(t_left[:, : 2 * s], s) + t_right[:, : 2 * s]
        sum_i = swap(t_left[:, 2 * s :], s) + t_right[:, 2 * s :]
        middle = split(jnp.where(below, sum_r, swap(sum_i, s)))
        ends = jnp.concatenate(
            [
                jnp.where(below, t_left[:, : 2 * s], t_right[:, : 2 * s]),
                jnp.where(below, t_left[:, 2 * s :], t_right[:, 2 * s :]),
            ],
            axis=1,
        )
        kept.append((dot(middle, pinv_emb), back, below))
        return ends - dot(middle, z_emb)

    y_all = None
    t = None
    for l in range(top):
        is_low = bits[l] == 0
        s_copies[l].wait_recv()
        mine, other = sbuf[l], sgot[l]
        left = jnp.where(is_low, mine, other)
        right = jnp.where(is_low, other, mine)
        lr, li = left[:, : 2 * s], left[:, 2 * s :]
        rr, ri = right[:, : 2 * s], right[:, 2 * s :]
        pivot = jnp.where(low, swap(lr[s:], s) + rr[:s], swap(swap(li[s:], s) + ri[:s], s))
        y_re = jnp.where(low, lr[s:], rr[:s])
        y_im = jnp.where(low, li[s:], ri[:s])
        turned = split(jnp.transpose(jnp.concatenate([y_re, y_im], axis=0)))
        y_emb = split(embed(y_re, y_im))
        base = jnp.concatenate(
            [
                jnp.concatenate([jnp.where(low, lr[:s], 0.0), jnp.where(low, li[:s], 0.0)], axis=1),
                jnp.concatenate([jnp.where(low, 0.0, rr[s:]), jnp.where(low, 0.0, ri[s:])], axis=1),
            ],
            axis=0,
        )
        pinv = inverse(pivot)
        z = dot(pinv, y_emb)
        z_re, z_im = z[:, : 2 * s], z[:, 2 * s :]
        z_emb = split(embed(z_re, z_im))
        merged = base - dot(turned, z_emb)
        back = split(
            jnp.concatenate(
                [jnp.concatenate([z_re, -z_im], axis=1), jnp.concatenate([z_im, z_re], axis=1)], axis=0
            )
        )
        if l + 1 < top:
            send_matrix(l + 1)
        if l == 0:
            t, y_all = start_rights()
            send_rights(0, t)
            if l + 1 < top:
                weighted = wr * green_ref[0] - wi * green_ref[1]
                first[...] = dot(weighted, y_all)
        if l + 1 < top:
            t = merge_rights(l, z_emb, embed_packed(pinv), back)
            send_rights(l + 1, t)
        last = (z_emb, pinv, back)
    if not top:
        t, y_all = start_rights()
    if top < 2:
        weighted = wr * green_ref[0] - wi * green_ref[1]
        first[...] = dot(weighted, y_all)

    upper = bits[top] == 1
    end_pivot = jnp.where(low, swap(merged[s:, : 2 * s], s), merged[s:, 2 * s :])
    end_row = jnp.where(low, merged[s:, : 2 * s], swap(merged[s:, 2 * s :], s))
    end_col = jnp.where(low, swap(merged[:s, : 2 * s], s), merged[:s, 2 * s :])
    near = jnp.where(low, merged[:s, : 2 * s], swap(merged[:s, 2 * s :], s))
    row_emb = split(embed_packed(end_row))
    end_inv = inverse(end_pivot)
    end_z = dot(end_inv, row_emb)
    end_emb = split(embed_packed(end_z))
    ebuf[...] = jnp.where(upper, near - dot(end_col, end_emb), end_pivot)
    s_copies.append(send(ebuf, egot, s_s.at[top], s_r.at[top], (pole, mates[top])))
    if top:
        z_emb, pinv, back = last
        t = merge_rights(top - 1, z_emb, embed_packed(pinv), back)
    width = t.shape[0]
    below = lanes_below((width, 2 * s), s)
    t_end = jnp.where(below, swap(t[:, : 2 * s], s), t[:, 2 * s :])
    t_near = jnp.where(below, t[:, : 2 * s], swap(t[:, 2 * s :], s))
    t_ends = split(t_end)
    send_rights(top, jnp.where(upper, t_near - dot(t_ends, end_emb), t_end))
    x_part = dot(t_ends, embed_packed(end_inv))
    end_back = split(jnp.concatenate([jnp.where(low, end_z, -end_z), swap(end_z, s)], axis=0))
    s_copies[top].wait_recv()
    middle_inv = split(embed_packed(inverse(ebuf[...] + egot[...])))
    t_copies[top].wait_recv()
    xsends[top][...] = dot(tbufs[top][bits[top]] + tgots[top][...], middle_inv)

    def trade(l):
        copy = send(xsends[l], xgots[l].at[bits[l]], x_s.at[l], x_r.at[l], (pole, mates[l]))
        x_copies.append(copy)
        return copy

    copy = trade(top)
    xgots[top][bits[top]] = xsends[top][...]
    copy.wait_recv()
    xm = xgots[top][...].reshape(width, 2 * s)
    xm_t = swap(xm, s)
    x_end = x_part - dot(xm, end_back, 1, 1)
    x_end_t = swap(x_end, s)
    zero = jnp.zeros_like(xm)
    x = jnp.where(
        upper,
        jnp.concatenate([jnp.where(below, xm, x_end_t), jnp.where(below, xm_t, x_end)], axis=1),
        jnp.concatenate([jnp.where(below, zero, xm_t), jnp.where(below, zero, xm)], axis=1),
    )
    for l in reversed(range(top)):
        part_m, back, below = kept[l]
        xm = part_m - dot(x, back, 1, 1)
        xr, xi = x[:, : 2 * s], x[:, 2 * s :]
        xm_t = swap(xm, s)
        x_left = jnp.concatenate([jnp.where(below, xr, xm_t), jnp.where(below, xi, xm)], axis=1)
        x_right = jnp.concatenate([jnp.where(below, xm, xr), jnp.where(below, xm_t, xi)], axis=1)
        is_low = bits[l] == 0
        xsends[l][...] = jnp.where(is_low, x_right, x_left)
        copy = trade(l)
        xgots[l][bits[l]] = jnp.where(is_low, x_left, x_right)
        if l:
            copy.wait_recv()
            x = xgots[l][...].reshape(-1, 4 * s)
    if not top:
        xgots[0 if top else 1][...] = x.reshape(2, wide, 4 * s)

    rows = ni // poles
    rows_sep = s // poles
    o_copies, p_copies, own_copies = [], [], []
    for turn in range(halves):
        half = bits[0] if turn == 0 else 1 - bits[0]
        columns = pl.ds(pl.multiple_of(half * wide, wide), wide)
        if turn and top:
            copy.wait_recv()
        xh = xgots[0 if top else 1][half]
        xhs = split(xh)
        for o, peer in enumerate(peers + [pole]):
            at = pl.ds(pl.multiple_of(peer * rows, rows), rows)
            part[turn, peer] = first[at, columns] + dot(maps[at, :], xhs, 1, 1)
            if o == len(peers):
                own_copies.append(fetch(part.at[turn, peer], got.at[o, :, columns], 6 + turn))
            else:
                o_copies.append(
                    send(
                        part.at[turn, peer], got.at[o, :, columns],
                        o_s.at[turn, o], o_r.at[turn, o], (peer, dom),
                    )
                )
        weighted_sep = jnp.transpose(wr * xh[:, : 2 * s] - wi * xh[:, 2 * s :])[s:]
        for q in range(poles):
            part_sep[q, :, columns] = weighted_sep[q * rows_sep : (q + 1) * rows_sep]
    for o, peer in enumerate(peers):
        p_copies.append(
            send(part_sep.at[peer], got_sep.at[o], p_s.at[o], p_r.at[o], (peer, dom))
        )
    own_copies.append(fetch(part_sep.at[pole], got_sep.at[len(peers)], 8))
    for copy in o_copies + p_copies:
        copy.wait_recv()
    for copy in own_copies:
        copy.wait()
    for copy in y_copies + s_copies + t_copies + x_copies + o_copies + p_copies:
        copy.wait_send()


def add_poles(got, got_sep, out_ref, outsep_ref):
    out_ref[...] = jnp.sum(got[...], axis=0)
    outsep_ref[...] = jnp.sum(got_sep[...], axis=0)


def shards(poles, doms, y_interior, y_separator, green, pole_data, coupling, sep_block, iface_rows):
    rows, m = y_interior.shape[1:]
    s = sep_block.shape[-1]
    ni = green.shape[-1]
    levels = doms.bit_length() - 1
    others = max(poles - 1, 1)
    b = iface_rows.shape[-1]
    hbm = pl.BlockSpec(memory_space=pl.ANY)
    dma = pltpu.SemaphoreType.DMA
    buf = lambda *shape: pltpu.VMEM(shape, f32)
    widths = [m >> (l + 1) for l in range(levels)]
    cols = [4 * s] * (levels - 1) + [2 * s]
    sizes = list(zip(widths, cols))
    out, out_sep = pl.pallas_call(
        functools.partial(kernel, poles, doms),
        out_shape=(
            jax.ShapeDtypeStruct((poles, rows, m), f32),
            jax.ShapeDtypeStruct((poles, s // poles, m), f32),
        ),
        in_specs=[hbm, hbm, hbm, pl.BlockSpec(memory_space=pltpu.SMEM), hbm, hbm, hbm],
        out_specs=(hbm, hbm),
        scratch_shapes=[
            buf(s, m),
            buf(2, ni, ni),
            buf(2, s, b),
            buf(s, s),
            pltpu.VMEM((2, b), jnp.int32),
            buf(poles, rows, m),
            buf(2, poles, rows, m // 2),
            buf(poles, s // poles, m),
            buf(max(levels - 1, 1), 2 * s, 4 * s),
            buf(max(levels - 1, 1), 2 * s, 4 * s),
            buf(s, 2 * s),
            buf(s, 2 * s),
            [buf(2, w, c) for w, c in sizes],
            [buf(w, c) for w, c in sizes],
            [buf(w, c) for w, c in sizes],
            [buf(2, w, c) for w, c in sizes] + [buf(2, m // 2, 4 * s)],
            buf(ni, m),
            buf(ni, 4 * s),
            dma((9,)),
            dma((others,)), dma((others,)),
            dma((levels,)), dma((levels,)),
            dma((levels,)), dma((levels,)),
            dma((levels,)), dma((levels,)),
            dma((2, others)), dma((2, others)),
            dma((others,)), dma((others,)),
        ],
        compiler_params=pltpu.CompilerParams(
            collective_id=0, has_side_effects=True, vmem_limit_bytes=56 * 1024 * 1024
        ),
    )(
        y_interior[0], y_separator[0], green[:, 0, 0], pole_data[:, 0], coupling[0], sep_block[0],
        iface_rows[0],
    )
    vmem = pl.BlockSpec(memory_space=pltpu.VMEM)
    out, out_sep = pl.pallas_call(
        add_poles,
        out_shape=(
            jax.ShapeDtypeStruct((rows, m), f32),
            jax.ShapeDtypeStruct((s // poles, m), f32),
        ),
        in_specs=[vmem, vmem],
        out_specs=(vmem, vmem),
        compiler_params=pltpu.CompilerParams(vmem_limit_bytes=56 * 1024 * 1024),
    )(out, out_sep)
    return out[None], out_sep[None]


def solution(mesh):
    return jax.shard_map(
        functools.partial(shards, mesh.shape["pole"], mesh.shape["dom"]),
        mesh=mesh,
        in_specs=(
            P("dom", "pole", None),
            P("dom", None, None),
            P(None, "pole", "dom", None, None),
            P(None, "pole"),
            P("dom", None, None, None),
            P("dom", None, None),
            P("dom", None, None),
        ),
        out_specs=(P("dom", "pole", None), P("dom", "pole", None)),
        check_vma=False,
    )
```

```python
import functools
import jax
import jax.numpy as jnp
from jax import lax
from jax.experimental import pallas as pl
from jax.experimental.pallas import tpu as pltpu
from jax.sharding import PartitionSpec as P

MESH = pl.DeviceIdType.MESH
f32 = jnp.float32


def split(value):
    high = value.astype(jnp.bfloat16)
    return high, (value - high.astype(f32)).astype(jnp.bfloat16)


def dot(a, b, ca=1, cb=0):
    a_high, a_low = a if isinstance(a, tuple) else split(a)
    b_high, b_low = b if isinstance(b, tuple) else split(b)

    def one(u, v):
        return lax.dot_general(u, v, (((ca,), (cb,)), ((), ())), preferred_element_type=f32)

    return one(a_high, b_high) + (one(a_high, b_low) + one(a_low, b_high))


def lanes_below(shape, limit):
    return lax.broadcasted_iota(jnp.int32, shape, 1) < limit


def swap(value, half):
    return pltpu.roll(value, half, 1)


def sweep_rows(dr, di, top, turned):
    n = len(dr)
    row = lax.broadcasted_iota(jnp.int32, top.shape, 0)
    for k in range(n):
        pr, pi = dr[k][k : k + 1], di[k][k : k + 1]
        scale = 1.0 / (pr * pr + pi * pi)
        qr, qi = pr * scale, -pi * scale
        here = row == k
        cr, ci = dr[k], di[k]

        def reduced(re, im):
            tr, ti = re[k : k + 1], im[k : k + 1]
            rr, ri = tr * qr - ti * qi, tr * qi + ti * qr
            return (
                jnp.where(here, rr, re - cr * rr + ci * ri),
                jnp.where(here, ri, im - cr * ri - ci * rr),
            )

        later = [reduced(dr[m], di[m]) for m in range(k + 1, n)]
        dr = dr[: k + 1] + [pair[0] for pair in later]
        di = di[: k + 1] + [pair[1] for pair in later]
        top, turned = reduced(top, turned)
    return top, turned


def inverse(packed):
    n = packed.shape[0]
    step, steps = 8, 4
    lane = lax.broadcasted_iota(jnp.int32, packed.shape, 1)
    within = lax.rem(lane, n)
    sign = jnp.where(lane[:step] < n, 1.0, -1.0)
    row = lax.broadcasted_iota(jnp.int32, (step, 2 * n), 0)

    def body(_, a):
        shape = a.shape
        for b in range(steps):
            at = b * step
            swept = (within >= at) & (within < at + step)
            unit = (lane[:step] == row + at).astype(f32)
            col_r = [jnp.broadcast_to(a[:, at + m : at + m + 1], shape) for m in range(step)]
            col_i = [jnp.broadcast_to(a[:, n + at + m : n + at + m + 1], shape) for m in range(step)]
            top = jnp.where(swept[:step], unit, a[at : at + step])
            turned = swap(top, n) * sign
            r, ri = sweep_rows(
                [c[at : at + step] for c in col_r], [c[at : at + step] for c in col_i], top, turned
            )
            rest = jnp.where(swept, 0.0, a)
            for m in range(step):
                rest = rest - col_r[m] * r[m : m + 1] + col_i[m] * ri[m : m + 1]
            pieces = [rest[:at], r, rest[at + step :]] if at else [r, rest[step:]]
            a = jnp.concatenate(pieces, axis=0)
        move = step * steps
        a = jnp.concatenate([a[move:], a[:move]], axis=0)
        return jnp.where(within < n - move, pltpu.roll(a, 2 * n - move, 1), pltpu.roll(a, n - move, 1))

    return lax.fori_loop(0, n // (step * steps), body, packed)


def embed(re, im):
    return jnp.concatenate(
        [jnp.concatenate([re, im], axis=1), jnp.concatenate([-im, re], axis=1)], axis=0
    )


def embed_packed(packed):
    n = packed.shape[1] // 2
    turned = swap(packed, n) * jnp.where(lanes_below(packed.shape, n), -1.0, 1.0)
    return jnp.concatenate([packed, turned], axis=0)


def kernel(
    poles, doms, y_hbm, ysep_hbm, green_hbm, pole_ref, coup_hbm, sep_hbm, rows_hbm,
    got, got_sep,
    ysep_ref, green_ref, coup_ref, sep_ref, rows_ref,
    ybuf, part, part_sep, sbuf, sgot, ebuf, egot, tbufs, tgots, xsends, xgots, first, maps,
    load, y_s, y_r, s_s, s_r, t_s, t_r, x_s, x_r, o_s, o_r, p_s, p_r,
):
    levels = doms.bit_length() - 1
    top = levels - 1
    pole = lax.axis_index("pole")
    dom = lax.axis_index("dom")
    bits = [lax.rem(lax.div(dom, 1 << l), 2) for l in range(levels)]
    mates = [dom + (1 - 2 * bits[l]) * (1 << l) for l in range(levels)]
    pole_bits = [lax.rem(lax.div(pole, 1 << b), 2) for b in range(poles.bit_length() - 1)]
    flips = sorted(range(1, poles), key=lambda o: (-bin(o).count("1"), o))
    peers = [
        pole + sum((1 - 2 * bit) * (1 << b) for b, bit in enumerate(pole_bits) if o >> b & 1)
        for o in flips
    ]

    def fetch(src, dst, number):
        copy = pltpu.make_async_copy(src, dst, load.at[number])
        copy.start()
        return copy

    def send(src, dst, send_sem, recv_sem, place):
        copy = pltpu.make_async_remote_copy(
            src_ref=src, dst_ref=dst, send_sem=send_sem, recv_sem=recv_sem,
            device_id=place, device_id_type=MESH,
        )
        copy.start()
        return copy

    loads = [
        fetch(rows_hbm, rows_ref, 0),
        fetch(coup_hbm, coup_ref, 1),
        fetch(green_hbm, green_ref, 2),
        fetch(sep_hbm, sep_ref, 3),
        fetch(y_hbm, ybuf.at[pole], 4),
        fetch(ysep_hbm, ysep_ref, 5),
    ]
    barrier = pltpu.get_barrier_semaphore()
    for peer in peers:
        pl.semaphore_signal(barrier, inc=1, device_id=(peer, dom), device_id_type=MESH)
    for mate in mates:
        pl.semaphore_signal(barrier, inc=1, device_id=(pole, mate), device_id_type=MESH)

    s = sep_ref.shape[0]
    ni = green_ref.shape[1]
    m = y_hbm.shape[1]
    zr, zi, wr, wi = pole_ref[0], pole_ref[1], pole_ref[2], pole_ref[3]
    for copy in loads[:2]:
        copy.wait()
    spot = lax.broadcasted_iota(jnp.int32, (ni, rows_ref.shape[1]), 0)
    pick_u = (spot == rows_ref[0:1]).astype(f32)
    pick_w = (spot == rows_ref[1:2]).astype(f32)
    has_left = (dom > 0).astype(f32)
    c = split(
        jnp.concatenate([dot(coup_ref[1] * has_left, pick_w, 1, 1), dot(coup_ref[0], pick_u, 1, 1)], axis=0)
    )
    for copy in loads[2:4]:
        copy.wait()
    n_r = dot(c, green_ref[0])
    n_i = dot(c, green_ref[1])
    n_rs, n_is = split(n_r), split(n_i)
    pl.semaphore_wait(barrier, len(peers) + len(mates))
    y_copies = [
        send(y_hbm, ybuf.at[pole], y_s.at[o], y_r.at[o], (peer, dom)) for o, peer in enumerate(peers)
    ]
    k_r = dot(n_rs, c, 1, 1)
    k_i = dot(n_is, c, 1, 1)
    eye = (
        lax.broadcasted_iota(jnp.int32, (s, s), 0) == lax.broadcasted_iota(jnp.int32, (s, s), 1)
    ).astype(f32)
    gap = jnp.zeros((s, s), f32)

    def place_corner(block):
        under = jnp.concatenate([gap, block], axis=1)
        return jnp.concatenate([jnp.zeros_like(under), under], axis=0)

    corner_r, corner_i = zr * eye - sep_ref[...], zi * eye
    merged = jnp.concatenate([place_corner(corner_r) - k_r, place_corner(corner_i) - k_i], axis=1)
    low = lanes_below((s, 2 * s), s)
    kept = []
    s_copies, t_copies, x_copies = [], [], []

    def send_matrix(l):
        sbuf[l] = merged
        s_copies.append(send(sbuf.at[l], sgot.at[l], s_s.at[l], s_r.at[l], (pole, mates[l])))

    def send_rights(l, t):
        width = t.shape[0] // 2
        tbufs[l][0] = t[:width]
        tbufs[l][1] = t[width:]
        t_copies.append(
            send(tbufs[l].at[1 - bits[l]], tgots[l], t_s.at[l], t_r.at[l], (pole, mates[l]))
        )

    if top:
        send_matrix(0)
    maps[:, : 2 * s] = jnp.transpose(wr * n_r - wi * n_i)
    maps[:, 2 * s :] = jnp.transpose(-(wr * n_i + wi * n_r))
    halves = 2
    wide = m // halves

    def start_rights():
        for copy in loads[4:]:
            copy.wait()
        for copy in y_copies:
            copy.wait_recv()
        y_all = split(ybuf[...].reshape(ni, m))
        right_r = jnp.transpose(dot(n_rs, y_all))
        right_i = jnp.transpose(dot(n_is, y_all))
        sep_t = jnp.transpose(jnp.concatenate([jnp.zeros((s, m), f32), ysep_ref[...]], axis=0))
        return jnp.concatenate([right_r + sep_t, right_i], axis=1), y_all

    def merge_rights(l, z_emb, pinv_emb, back):
        t_copies[l].wait_recv()
        width = tgots[l].shape[0]
        is_low = bits[l] == 0
        t_mine, t_other = tbufs[l][bits[l]], tgots[l][...]
        t_left = jnp.where(is_low, t_mine, t_other)
        t_right = jnp.where(is_low, t_other, t_mine)
        below = lanes_below((width, 2 * s), s)
        sum_r = swap(t_left[:, : 2 * s], s) + t_right[:, : 2 * s]
        sum_i = swap(t_left[:, 2 * s :], s) + t_right[:, 2 * s :]
        middle = split(jnp.where(below, sum_r, swap(sum_i, s)))
        ends = jnp.concatenate(
            [
                jnp.where(below, t_left[:, : 2 * s], t_right[:, : 2 * s]),
                jnp.where(below, t_left[:, 2 * s :], t_right[:, 2 * s :]),
            ],
            axis=1,
        )
        kept.append((dot(middle, pinv_emb), back, below))
        return ends - dot(middle, z_emb)

    y_all = None
    t = None
    for l in range(top):
        is_low = bits[l] == 0
        s_copies[l].wait_recv()
        mine, other = sbuf[l], sgot[l]
        left = jnp.where(is_low, mine, other)
        right = jnp.where(is_low, other, mine)
        lr, li = left[:, : 2 * s], left[:, 2 * s :]
        rr, ri = right[:, : 2 * s], right[:, 2 * s :]
        pivot = jnp.where(low, swap(lr[s:], s) + rr[:s], swap(swap(li[s:], s) + ri[:s], s))
        y_re = jnp.where(low, lr[s:], rr[:s])
        y_im = jnp.where(low, li[s:], ri[:s])
        turned = split(jnp.transpose(jnp.concatenate([y_re, y_im], axis=0)))
        y_emb = split(embed(y_re, y_im))
        base = jnp.concatenate(
            [
                jnp.concatenate([jnp.where(low, lr[:s], 0.0), jnp.where(low, li[:s], 0.0)], axis=1),
                jnp.concatenate([jnp.where(low, 0.0, rr[s:]), jnp.where(low, 0.0, ri[s:])], axis=1),
            ],
            axis=0,
        )
        pinv = inverse(pivot)
        z = dot(pinv, y_emb)
        z_re, z_im = z[:, : 2 * s], z[:, 2 * s :]
        z_emb = split(embed(z_re, z_im))
        merged = base - dot(turned, z_emb)
        back = split(
            jnp.concatenate(
                [jnp.concatenate([z_re, -z_im], axis=1), jnp.concatenate([z_im, z_re], axis=1)], axis=0
            )
        )
        if l + 1 < top:
            send_matrix(l + 1)
        if l == 0:
            t, y_all = start_rights()
            send_rights(0, t)
            if l + 1 < top:
                weighted = wr * green_ref[0] - wi * green_ref[1]
                first[...] = dot(weighted, y_all)
        if l + 1 < top:
            t = merge_rights(l, z_emb, embed_packed(pinv), back)
            send_rights(l + 1, t)
        last = (z_emb, pinv, back)
    if not top:
        t, y_all = start_rights()
    if top < 2:
        weighted = wr * green_ref[0] - wi * green_ref[1]
        first[...] = dot(weighted, y_all)

    upper = bits[top] == 1
    end_pivot = jnp.where(low, swap(merged[s:, : 2 * s], s), merged[s:, 2 * s :])
    end_row = jnp.where(low, merged[s:, : 2 * s], swap(merged[s:, 2 * s :], s))
    end_col = jnp.where(low, swap(merged[:s, : 2 * s], s), merged[:s, 2 * s :])
    near = jnp.where(low, merged[:s, : 2 * s], swap(merged[:s, 2 * s :], s))
    row_emb = split(embed_packed(end_row))
    end_inv = inverse(end_pivot)
    end_z = dot(end_inv, row_emb)
    end_emb = split(embed_packed(end_z))
    ebuf[...] = jnp.where(upper, near - dot(end_col, end_emb), end_pivot)
    s_copies.append(send(ebuf, egot, s_s.at[top], s_r.at[top], (pole, mates[top])))
    if top:
        z_emb, pinv, back = last
        t = merge_rights(top - 1, z_emb, embed_packed(pinv), back)
    width = t.shape[0]
    below = lanes_below((width, 2 * s), s)
    t_end = jnp.where(below, swap(t[:, : 2 * s], s), t[:, 2 * s :])
    t_near = jnp.where(below, t[:, : 2 * s], swap(t[:, 2 * s :], s))
    t_ends = split(t_end)
    send_rights(top, jnp.where(upper, t_near - dot(t_ends, end_emb), t_end))
    x_part = dot(t_ends, embed_packed(end_inv))
    end_back = split(jnp.concatenate([jnp.where(low, end_z, -end_z), swap(end_z, s)], axis=0))
    s_copies[top].wait_recv()
    middle_inv = split(embed_packed(inverse(ebuf[...] + egot[...])))
    t_copies[top].wait_recv()
    xsends[top][...] = dot(tbufs[top][bits[top]] + tgots[top][...], middle_inv)

    def trade(l):
        copy = send(xsends[l], xgots[l].at[bits[l]], x_s.at[l], x_r.at[l], (pole, mates[l]))
        x_copies.append(copy)
        return copy

    copy = trade(top)
    xgots[top][bits[top]] = xsends[top][...]
    copy.wait_recv()
    xm = xgots[top][...].reshape(width, 2 * s)
    xm_t = swap(xm, s)
    x_end = x_part - dot(xm, end_back, 1, 1)
    x_end_t = swap(x_end, s)
    zero = jnp.zeros_like(xm)
    x = jnp.where(
        upper,
        jnp.concatenate([jnp.where(below, xm, x_end_t), jnp.where(below, xm_t, x_end)], axis=1),
        jnp.concatenate([jnp.where(below, zero, xm_t), jnp.where(below, zero, xm)], axis=1),
    )
    for l in reversed(range(top)):
        part_m, back, below = kept[l]
        xm = part_m - dot(x, back, 1, 1)
        xr, xi = x[:, : 2 * s], x[:, 2 * s :]
        xm_t = swap(xm, s)
        x_left = jnp.concatenate([jnp.where(below, xr, xm_t), jnp.where(below, xi, xm)], axis=1)
        x_right = jnp.concatenate([jnp.where(below, xm, xr), jnp.where(below, xm_t, xi)], axis=1)
        is_low = bits[l] == 0
        xsends[l][...] = jnp.where(is_low, x_right, x_left)
        copy = trade(l)
        xgots[l][bits[l]] = jnp.where(is_low, x_left, x_right)
        if l:
            copy.wait_recv()
            x = xgots[l][...].reshape(-1, 4 * s)
    if not top:
        xgots[0 if top else 1][...] = x.reshape(2, wide, 4 * s)

    rows = ni // poles
    rows_sep = s // poles
    o_copies, p_copies, own_copies = [], [], []
    for turn in range(halves):
        half = bits[0] if turn == 0 else 1 - bits[0]
        columns = pl.ds(pl.multiple_of(half * wide, wide), wide)
        if turn and top:
            copy.wait_recv()
        xh = xgots[0 if top else 1][half]
        xhs = split(xh)
        for o, peer in enumerate(peers + [pole]):
            at = pl.ds(pl.multiple_of(peer * rows, rows), rows)
            part[turn, peer] = first[at, columns] + dot(maps[at, :], xhs, 1, 1)
            if o == len(peers):
                own_copies.append(fetch(part.at[turn, peer], got.at[o, :, columns], 6 + turn))
            else:
                o_copies.append(
                    send(
                        part.at[turn, peer], got.at[o, :, columns],
                        o_s.at[turn, o], o_r.at[turn, o], (peer, dom),
                    )
                )
        weighted_sep = jnp.transpose(wr * xh[:, : 2 * s] - wi * xh[:, 2 * s :])[s:]
        for q in range(poles):
            part_sep[q, :, columns] = weighted_sep[q * rows_sep : (q + 1) * rows_sep]
    for o, peer in enumerate(peers):
        p_copies.append(
            send(part_sep.at[peer], got_sep.at[o], p_s.at[o], p_r.at[o], (peer, dom))
        )
    own_copies.append(fetch(part_sep.at[pole], got_sep.at[len(peers)], 8))
    for copy in o_copies + p_copies:
        copy.wait_recv()
    for copy in own_copies:
        copy.wait()
    for copy in y_copies + s_copies + t_copies + x_copies + o_copies + p_copies:
        copy.wait_send()


def add_poles(got, got_sep, out_ref, outsep_ref):
    out_ref[...] = jnp.sum(got[...], axis=0)
    outsep_ref[...] = jnp.sum(got_sep[...], axis=0)


def shards(poles, doms, y_interior, y_separator, green, pole_data, coupling, sep_block, iface_rows):
    rows, m = y_interior.shape[1:]
    s = sep_block.shape[-1]
    ni = green.shape[-1]
    levels = doms.bit_length() - 1
    others = max(poles - 1, 1)
    b = iface_rows.shape[-1]
    hbm = pl.BlockSpec(memory_space=pl.ANY)
    dma = pltpu.SemaphoreType.DMA
    buf = lambda *shape: pltpu.VMEM(shape, f32)
    widths = [m >> (l + 1) for l in range(levels)]
    cols = [4 * s] * (levels - 1) + [2 * s]
    sizes = list(zip(widths, cols))
    out, out_sep = pl.pallas_call(
        functools.partial(kernel, poles, doms),
        out_shape=(
            jax.ShapeDtypeStruct((poles, rows, m), f32),
            jax.ShapeDtypeStruct((poles, s // poles, m), f32),
        ),
        in_specs=[hbm, hbm, hbm, pl.BlockSpec(memory_space=pltpu.SMEM), hbm, hbm, hbm],
        out_specs=(hbm, hbm),
        scratch_shapes=[
            buf(s, m),
            buf(2, ni, ni),
            buf(2, s, b),
            buf(s, s),
            pltpu.VMEM((2, b), jnp.int32),
            buf(poles, rows, m),
            buf(2, poles, rows, m // 2),
            buf(poles, s // poles, m),
            buf(max(levels - 1, 1), 2 * s, 4 * s),
            buf(max(levels - 1, 1), 2 * s, 4 * s),
            buf(s, 2 * s),
            buf(s, 2 * s),
            [buf(2, w, c) for w, c in sizes],
            [buf(w, c) for w, c in sizes],
            [buf(w, c) for w, c in sizes],
            [buf(2, w, c) for w, c in sizes] + [buf(2, m // 2, 4 * s)],
            buf(ni, m),
            buf(ni, 4 * s),
            dma((9,)),
            dma((others,)), dma((others,)),
            dma((levels,)), dma((levels,)),
            dma((levels,)), dma((levels,)),
            dma((levels,)), dma((levels,)),
            dma((2, others)), dma((2, others)),
            dma((others,)), dma((others,)),
        ],
        compiler_params=pltpu.CompilerParams(
            collective_id=0, has_side_effects=True, vmem_limit_bytes=56 * 1024 * 1024
        ),
    )(
        y_interior[0], y_separator[0], green[:, 0, 0], pole_data[:, 0], coupling[0], sep_block[0],
        iface_rows[0],
    )
    vmem = pl.BlockSpec(memory_space=pltpu.VMEM)
    out, out_sep = pl.pallas_call(
        add_poles,
        out_shape=(
            jax.ShapeDtypeStruct((rows, m), f32),
            jax.ShapeDtypeStruct((s // poles, m), f32),
        ),
        in_specs=[vmem, vmem],
        out_specs=(vmem, vmem),
        compiler_params=pltpu.CompilerParams(vmem_limit_bytes=56 * 1024 * 1024),
    )(out, out_sep)
    return out[None], out_sep[None]


def solution(mesh):
    return jax.shard_map(
        functools.partial(shards, mesh.shape["pole"], mesh.shape["dom"]),
        mesh=mesh,
        in_specs=(
            P("dom", "pole", None),
            P("dom", None, None),
            P(None, "pole", "dom", None, None),
            P(None, "pole"),
            P("dom", None, None, None),
            P("dom", None, None),
            P("dom", None, None),
        ),
        out_specs=(P("dom", "pole", None), P("dom", "pole", None)),
        check_vma=False,
    )
```
